128 devices in a mesh: src: 32 (over y, z, core), tgt: 4 (over x).
Axes of the slice: x: 4, y: 4, z: 4, core: 2. Of those that a mesh axis runs over, the one named last changes fastest.
Arguments:
- src_points: float32 [32, 16384], P(None, 'src'), may hold values from -10 to 10
- tgt_points: float32 [32, 65536], P(None, 'tgt'), may hold values from -10 to 10
Outputs:
- source_dual: float32 [16384], P('src')
- target_dual: float32 [65536], P('tgt')
- mapped_targets: float32 [32, 65536], P(None, 'tgt')
The draws below stay inside these ranges and needn't reach their ends.
All inputs are finite; a program needn't handle non-finite values.
Results may differ from the reference program's by a relative error of at most 0.0003.
Values sent between devices are 32-bit elements; how exact they have to be, the bound alone decides.
No kernel may reach another device: no remote copies, remote signals or barrier semaphores. Data moves between devices by JAX's collectives and lax.ppermute only.
A program may use at most 192 MiB of HBM per device.

```python
import math
import jax
import jax.numpy as jnp
from jax import lax

DIM = 32
ITERS = 2
NS = 16384
NT = 65536


def draw_src_points(key, part):
    key = jax.random.fold_in(key, 11)
    first = jax.random.fold_in(key, 0)
    values = jax.random.truncated_normal(first, -6.0, 6.0, (DIM, NS), jnp.float32) * 0.5
    return values


def draw_tgt_points(key, part):
    key = jax.random.fold_in(key, 23)
    first = jax.random.fold_in(key, 0)
    values = jax.random.truncated_normal(first, -6.0, 6.0, (DIM, NT), jnp.float32) * 0.5
    return values


def setup_inputs(seed: int = 0) -> dict:
    streams_of = jax.random.split(jax.random.key(seed), 3)
    src_points = draw_src_points(jax.random.fold_in(streams_of[2], 71), 0)
    tgt_points = draw_tgt_points(jax.random.fold_in(streams_of[2], 71), 0)
    return dict(src_points=src_points, tgt_points=tgt_points)


EPSILON = 0.5


def cost_block(src_points, src_sq, tgt_block):
    cross = lax.dot_general(src_points, tgt_block, (((0,), (0,)), ((), ())), precision=lax.Precision.HIGHEST, preferred_element_type=jnp.float32)
    tgt_sq = jnp.sum(tgt_block * tgt_block, axis=0)
    return src_sq[:, None] + tgt_sq[None, :] - 2.0 * cross


def reference(src_points, tgt_points):
    width_block = min(2048, NT)
    block_count = NT // width_block
    log_src = -math.log(NS)
    log_tgt = -math.log(NT)
    src_sq = jnp.sum(src_points * src_points, axis=0)
    tgt_blocks = tgt_points.reshape(DIM, block_count, width_block).transpose(1, 0, 2)

    def row_dual(dual_tgt):
        def visit(carry, items):
            tgt_block, dual_block = items
            scores = (dual_block[None, :] - cost_block(src_points, src_sq, tgt_block)) / EPSILON + log_tgt
            peak = jnp.max(scores, axis=1)
            newest = jnp.maximum(carry[0], peak)
            total = carry[1] * jnp.exp(carry[0] - newest) + jnp.sum(jnp.exp(scores - newest[:, None]), axis=1)
            return (newest, total), None

        start = (jnp.full((NS,), -jnp.inf, jnp.float32), jnp.zeros((NS,), jnp.float32))
        (peak, total), _ = lax.scan(visit, start, (tgt_blocks, dual_tgt))
        return -EPSILON * (peak + jnp.log(total))

    def col_dual(dual_src):
        def visit(tgt_block):
            scores = (dual_src[:, None] - cost_block(src_points, src_sq, tgt_block)) / EPSILON + log_src
            peak = jnp.max(scores, axis=0)
            total = jnp.sum(jnp.exp(scores - peak[None, :]), axis=0)
            return -EPSILON * (peak + jnp.log(total))

        return lax.map(visit, tgt_blocks)

    dual_tgt = jnp.zeros((block_count, width_block), jnp.float32)
    dual_src = jnp.zeros((NS,), jnp.float32)
    for iteration in range(ITERS):
        dual_src = row_dual(dual_tgt)
        dual_tgt = col_dual(dual_src)

    def weigh(items):
        tgt_block, dual_block = items
        weights = jnp.exp((dual_src[:, None] + dual_block[None, :] - cost_block(src_points, src_sq, tgt_block)) / EPSILON + log_src)
        return jnp.dot(src_points, weights, precision=lax.Precision.HIGHEST, preferred_element_type=jnp.float32)

    moments = lax.map(weigh, (tgt_blocks, dual_tgt))
    mapped = moments.transpose(1, 0, 2).reshape(DIM, NT)
    return dual_src, dual_tgt.reshape(NT), mapped
```

```python
import functools
import math

import jax
import jax.numpy as jnp
from jax import lax
from jax.experimental import pallas as pl
from jax.experimental.pallas import tpu as pltpu
from jax.sharding import PartitionSpec as P

EPSILON = 0.5
LOG2E = 1.4426950408889634
UNIT = LOG2E / EPSILON
BF = jnp.bfloat16
F32 = jnp.float32
DEPTH = 256
VMEM_LIMIT = 56 * 2**20


def params():
    return pltpu.CompilerParams(vmem_limit_bytes=VMEM_LIMIT)


def log2(a):
    return jnp.log(a) * LOG2E


def split3(a):
    a1 = a.astype(BF)
    rest = a - a1.astype(F32)
    a2 = rest.astype(BF)
    rest = rest - a2.astype(F32)
    return a1, a2, rest.astype(BF)


def square_norm(points):
    return jnp.sum(points * points, axis=0, keepdims=True)


def build_still(points, term, out):
    n = points.shape[1]
    p1, p2, p3 = (p.astype(F32) for p in split3(points * (2 * UNIT)))
    t1, t2, t3 = (t.astype(F32) for t in split3(term))
    ones = jnp.ones((3, n), F32)
    zeros = jnp.zeros((DEPTH - 198, n), F32)
    whole = jnp.concatenate([p1, p1, p1, p2, p2, p3, t1, t2, t3, ones, zeros], axis=0)
    out[...] = whole.T.astype(BF)


def build_moving(points, term, out):
    n = points.shape[1]
    p1, p2, p3 = split3(points)
    t1, t2, t3 = (t.astype(F32) for t in split3(term))
    for row, part in enumerate((p1, p2, p3, p1, p2, p1)):
        out[32 * row : 32 * row + 32, :] = part
    ones, zeros = jnp.ones((3, n), F32), jnp.zeros((10, n), F32)
    out[192:208, :] = jnp.concatenate([ones, t1, t2, t3, zeros], axis=0).astype(BF)


def tree(op, items):
    items = list(items)
    while len(items) > 1:
        items = [op(a, b) for a, b in zip(items[::2], items[1::2])] + items[len(items) & ~1 :]
    return items[0]


def lanes(block):
    return jnp.concatenate([block[k : k + 1, :] for k in range(block.shape[0])], axis=1)


def rows(line):
    return jnp.concatenate([line[:, k : k + 128] for k in range(0, line.shape[1], 128)], axis=0)


def sweep(steps, make, multiply, process):
    make(0, 0)
    multiply(0)
    make(1, 1)

    def pair(t, carry):
        multiply(1)
        make(lax.rem(2 * t + 2, steps), 0)
        process(2 * t, 0)
        multiply(0)
        make(lax.rem(2 * t + 3, steps), 1)
        process(2 * t + 1, 1)
        return carry

    lax.fori_loop(0, steps // 2, pair, 0)


def row_first_kernel(tile, x_ref, y_ref, out, still, moving, scores, peak, total):
    count = x_ref.shape[1]
    x = x_ref[...]
    build_still(x, -UNIT * square_norm(x), still)
    moving[:, 208:DEPTH, :] = jnp.zeros((2, DEPTH - 208, tile), BF)
    peak[...] = jnp.full(peak.shape, -1e30, F32)
    total[...] = jnp.zeros(total.shape, F32)

    def make(t, slot):
        y = y_ref[:, pl.ds(pl.multiple_of(t * tile, tile), tile)]
        build_moving(y, -UNIT * square_norm(y), moving.at[slot])

    def multiply(slot):
        scores[slot] = jnp.dot(still[...], moving[slot], preferred_element_type=F32)

    def process(t, slot):
        for r in range(0, count, 8):
            s = [scores[slot, r : r + 8, k : k + 128] for k in range(0, tile, 128)]
            old = peak[r : r + 8, :]
            new = jnp.maximum(old, tree(jnp.maximum, s))
            part = tree(jnp.add, [jnp.exp2(a - new) for a in s])
            total[r : r + 8, :] = total[r : r + 8, :] * jnp.exp2(old - new) + part
            peak[r : r + 8, :] = new

    sweep(y_ref.shape[1] // tile, make, multiply, process)
    peaks = peak[...].T
    top = jnp.max(peaks, axis=0, keepdims=True)
    whole = jnp.sum(total[...].T * jnp.exp2(peaks - top), axis=0, keepdims=True)
    out[...] = jnp.concatenate([rows(top), rows(whole)], axis=0)


def row_first(x, y):
    tile, count = 1024, x.shape[1]
    return pl.pallas_call(
        functools.partial(row_first_kernel, tile),
        out_shape=jax.ShapeDtypeStruct((8, 128), F32),
        scratch_shapes=[
            pltpu.VMEM((count, DEPTH), BF),
            pltpu.VMEM((2, DEPTH, tile), BF),
            pltpu.VMEM((2, count, tile), F32),
            pltpu.VMEM((count, 128), F32),
            pltpu.VMEM((count, 128), F32),
        ],
        compiler_params=params(),
        name="row_first",
    )(x, y)


def col_first_kernel(tile, log_b, x_ref, y_ref, a0, a1, a2, a3, out, dual_out, still, moving, scores):
    count = x_ref.shape[1]
    parts = [a[...] for a in (a0, a1, a2, a3)]
    top = tree(jnp.maximum, [p[0:4] for p in parts])
    whole = tree(jnp.add, [p[4:8] * jnp.exp2(p[0:4] - top) for p in parts])
    dual = -(top + log2(whole) + log_b)
    dual_out[...] = dual
    x = x_ref[...]
    build_still(x, lanes(dual) - UNIT * square_norm(x), still)
    moving[:, 208:DEPTH, :] = jnp.zeros((2, DEPTH - 208, tile), BF)

    def make(t, slot):
        y = y_ref[:, pl.ds(pl.multiple_of(t * tile, tile), tile)]
        build_moving(y, -UNIT * square_norm(y), moving.at[slot])

    def multiply(slot):
        scores[slot] = jnp.dot(still[...], moving[slot], preferred_element_type=F32)

    def process(t, slot):
        tops, sums = [], []
        for k in range(0, tile, 128):
            peak = total = None
            for c in range(0, count, 128):
                s = [scores[slot, r : r + 8, k : k + 128] for r in range(c, c + 128, 8)]
                new = tree(jnp.maximum, s)
                if c:
                    new = jnp.maximum(peak, new)
                part = tree(jnp.add, [jnp.exp2(a - new) for a in s])
                total = total * jnp.exp2(peak - new) + part if c else part
                peak = new
            best = jnp.max(peak, axis=0, keepdims=True)
            tops.append(best)
            sums.append(jnp.sum(total * jnp.exp2(peak - best), axis=0, keepdims=True))
        out[t] = jnp.concatenate(tops + sums, axis=0)

    sweep(y_ref.shape[1] // tile, make, multiply, process)


def col_first(x, y, parts, log_b):
    tile, count = 512, x.shape[1]
    steps = y.shape[1] // tile
    return pl.pallas_call(
        functools.partial(col_first_kernel, tile, log_b),
        out_shape=(
            jax.ShapeDtypeStruct((steps, 8, 128), F32),
            jax.ShapeDtypeStruct((4, 128), F32),
        ),
        scratch_shapes=[
            pltpu.VMEM((count, DEPTH), BF),
            pltpu.VMEM((2, DEPTH, tile), BF),
            pltpu.VMEM((2, count, tile), F32),
        ],
        compiler_params=params(),
        name="col_first",
    )(x, y, *parts)


def join_targets_kernel(log_a, in_ref, own, out):
    top = in_ref[0, 0:4]
    for s in range(1, in_ref.shape[0]):
        top = jnp.maximum(top, in_ref[s, 0:4])
    whole = jnp.zeros((4, 128), F32)
    for s in range(in_ref.shape[0]):
        whole = whole + in_ref[s, 4:8] * jnp.exp2(in_ref[s, 0:4] - top)
    dual = -(top + log2(whole) + log_a)
    own[...] = dual
    for s in range(out.shape[0]):
        out[s] = dual


def join_targets(parts, log_a):
    return pl.pallas_call(
        functools.partial(join_targets_kernel, log_a),
        out_shape=(
            jax.ShapeDtypeStruct((4, 128), F32),
            jax.ShapeDtypeStruct((parts.shape[0], 4, 128), F32),
        ),
        compiler_params=params(),
        name="join_targets",
    )(parts)


def row_second_kernel(tile, log_b, x_ref, y_ref, f_ref, g_ref, out, still, moving, scores, total):
    count = x_ref.shape[1]
    x = x_ref[...]
    build_still(x, lanes(f_ref[...]) - UNIT * square_norm(x), still)
    moving[:, 208:DEPTH, :] = jnp.zeros((2, DEPTH - 208, tile), BF)
    total[...] = jnp.zeros(total.shape, F32)
    group = tile // 128

    def make(t, slot):
        y = y_ref[:, pl.ds(pl.multiple_of(t * tile, tile), tile)]
        g = lanes(g_ref[pl.ds(pl.multiple_of(t * group, group), group), :])
        build_moving(y, g + log_b - UNIT * square_norm(y), moving.at[slot])

    def multiply(slot):
        scores[slot] = jnp.dot(still[...], moving[slot], preferred_element_type=F32)

    def process(t, slot):
        for r in range(0, count, 8):
            e = [jnp.exp2(scores[slot, r : r + 8, k : k + 128]) for k in range(0, tile, 128)]
            total[r : r + 8, :] += tree(jnp.add, e)

    sweep(y_ref.shape[1] // tile, make, multiply, process)
    out[...] = rows(jnp.sum(total[...].T, axis=0, keepdims=True))


def row_second(x, y, f, g, log_b):
    tile, count = 1024, x.shape[1]
    return pl.pallas_call(
        functools.partial(row_second_kernel, tile, log_b),
        out_shape=jax.ShapeDtypeStruct((4, 128), F32),
        scratch_shapes=[
            pltpu.VMEM((count, DEPTH), BF),
            pltpu.VMEM((2, DEPTH, tile), BF),
            pltpu.VMEM((2, count, tile), F32),
            pltpu.VMEM((count, 128), F32),
        ],
        compiler_params=params(),
        name="row_second",
    )(x, y, f, g)


def join_sources_kernel(f_ref, a0, a1, a2, a3, own, out):
    whole = (a0[...] + a1[...]) + (a2[...] + a3[...])
    dual = f_ref[...] - log2(whole)
    own[...] = dual * (1.0 / UNIT)
    for s in range(out.shape[0]):
        out[s] = dual


def join_sources(f, parts, copies):
    return pl.pallas_call(
        join_sources_kernel,
        out_shape=(
            jax.ShapeDtypeStruct((4, 128), F32),
            jax.ShapeDtypeStruct((copies, 4, 128), F32),
        ),
        compiler_params=params(),
        name="join_sources",
    )(f, *parts)


def col_second_kernel(log_a, x_ref, f_ref, y_ref, g_ref, out, still, moving, scores, weights, values, total):
    tile = x_ref.shape[2]
    count = y_ref.shape[1]
    y = y_ref[...]
    g = g_ref[...]
    build_still(y, lanes(g) + log_a - UNIT * square_norm(y), still)
    moving[:, 208:DEPTH, :] = jnp.zeros((2, DEPTH - 208, tile), BF)
    values[:, 96:128, :] = jnp.ones((2, 32, 2 * tile), BF)
    total[...] = jnp.zeros(total.shape, F32)

    def make(t, slot):
        x = x_ref[t]
        f = lanes(f_ref[t])
        build_moving(x, f - UNIT * square_norm(x), moving.at[slot])

    def multiply(slot):
        scores[slot] = jnp.dot(still[...], moving[slot], preferred_element_type=F32)

    def process(t, slot):
        for part in range(3):
            piece = moving[slot, 32 * part : 32 * part + 32, :]
            values[slot, 32 * part : 32 * part + 32, 0:tile] = piece
            values[slot, 32 * part : 32 * part + 32, tile : 2 * tile] = piece
        for r in range(0, count, 16):
            for k in range(0, tile, 128):
                e = jnp.exp2(scores[slot, r : r + 16, k : k + 128])
                high = e.astype(BF)
                weights[slot, r : r + 16, k : k + 128] = high
                weights[slot, r : r + 16, tile + k : tile + k + 128] = (e - high.astype(F32)).astype(BF)
        total[...] += lax.dot_general(
            weights[slot], values[slot], (((1,), (1,)), ((), ())), preferred_element_type=F32
        )

    steps = x_ref.shape[0]
    make(0, 0)
    multiply(0)

    def pair(t, carry):
        make(2 * t + 1, 1)
        multiply(1)
        process(2 * t, 0)
        make(lax.rem(2 * t + 2, steps), 0)
        multiply(0)
        process(2 * t + 1, 1)
        return carry

    lax.fori_loop(0, steps // 2, pair, 0)
    sums = total[...].T
    weight = sums[96:97, :]
    mapped = (sums[0:32] + sums[32:64] + sums[64:96]) / weight
    for k in range(4):
        out[32 * k : 32 * k + 32, :] = mapped[:, 128 * k : 128 * k + 128]
    out[128:132, :] = (g - rows(log2(weight))) * (1.0 / UNIT)
    out[132:136, :] = jnp.zeros((4, 128), F32)


def col_second(x, f, y, g, log_a):
    steps, dims, tile = x.shape
    count = y.shape[1]
    return pl.pallas_call(
        functools.partial(col_second_kernel, log_a),
        out_shape=jax.ShapeDtypeStruct((136, 128), F32),
        scratch_shapes=[
            pltpu.VMEM((count, DEPTH), BF),
            pltpu.VMEM((2, DEPTH, tile), BF),
            pltpu.VMEM((2, count, tile), F32),
            pltpu.VMEM((2, count, 2 * tile), BF),
            pltpu.VMEM((2, 128, 2 * tile), BF),
            pltpu.VMEM((count, 128), F32),
        ],
        compiler_params=params(),
        name="col_second",
    )(x, f, y, g)


def unpack_kernel(in_ref, mapped, dual):
    for b in range(in_ref.shape[0]):
        for k in range(4):
            column = 512 * b + 128 * k
            mapped[:, column : column + 128] = in_ref[b, 32 * k : 32 * k + 32, :]
        dual[4 * b : 4 * b + 4, :] = in_ref[b, 128:132, :]


def unpack(parts):
    blocks, group = parts.shape[0], 8
    return pl.pallas_call(
        unpack_kernel,
        grid=(blocks // group,),
        in_specs=[pl.BlockSpec((group, 136, 128), lambda b: (b, 0, 0))],
        out_specs=(
            pl.BlockSpec((32, 512 * group), lambda b: (0, b)),
            pl.BlockSpec((4 * group, 128), lambda b: (b, 0)),
        ),
        out_shape=(
            jax.ShapeDtypeStruct((32, 512 * blocks), F32),
            jax.ShapeDtypeStruct((4 * blocks, 128), F32),
        ),
        compiler_params=params(),
        name="unpack",
    )(parts)


def over_tgt(part):
    n = lax.axis_size("tgt")
    turns = [[(i, (i + k) % n) for i in range(n)] for k in (1, 3, 2)]
    return [part] + [lax.ppermute(part, "tgt", turn) for turn in turns]


def body(x, y):
    sources, columns = lax.axis_size("src"), y.shape[1]
    log_a = -math.log2(x.shape[1] * sources)
    log_b = -math.log2(columns * lax.axis_size("tgt"))
    me = lax.axis_index("src")
    every_x = lax.all_gather(x, "src")
    own_y = lax.dynamic_slice_in_dim(y, me * (columns // sources), columns // sources, axis=1)

    first = over_tgt(row_first(x, y))
    partial, f1 = col_first(x, y, first, log_b)
    partial = lax.all_to_all(partial, "src", 0, 0)
    own_g, copies = join_targets(partial, log_a)
    g1 = lax.all_to_all(copies, "src", 0, 0)
    second = over_tgt(row_second(x, y, f1, g1.reshape(4 * sources, 128), log_b))
    source_dual, copies = join_sources(f1, second, sources)
    f2 = lax.all_to_all(copies, "src", 0, 0)
    block = col_second(every_x, f2, own_y, own_g, log_a)
    blocks = lax.all_to_all(jnp.broadcast_to(block[None], (sources, 136, 128)), "src", 0, 0)
    mapped, target_dual = unpack(blocks)
    return source_dual.reshape(-1), target_dual.reshape(-1), mapped


def solution(mesh):
    return jax.shard_map(
        body,
        mesh=mesh,
        in_specs=(P(None, "src"), P(None, "tgt")),
        out_specs=(P("src"), P("tgt"), P(None, "tgt")),
        check_vma=False,
    )
```

```python
import functools
import math

import jax
import jax.numpy as jnp
from jax import lax
from jax.experimental import pallas as pl
from jax.experimental.pallas import tpu as pltpu
from jax.sharding import Mesh
from jax.sharding import PartitionSpec as P

EPSILON = 0.5
LOG2E = 1.4426950408889634
UNIT = LOG2E / EPSILON
BF = jnp.bfloat16
F32 = jnp.float32
DEPTH = 256
VMEM_LIMIT = 56 * 2**20


def params():
    return pltpu.CompilerParams(vmem_limit_bytes=VMEM_LIMIT)


def log2(a):
    return jnp.log(a) * LOG2E


def split3(a):
    a1 = a.astype(BF)
    rest = a - a1.astype(F32)
    a2 = rest.astype(BF)
    rest = rest - a2.astype(F32)
    return a1, a2, rest.astype(BF)


def square_norm(points):
    return jnp.sum(points * points, axis=0, keepdims=True)


def build_still(points, term, out, shift=None):
    n = points.shape[1]
    p1, p2, p3 = (p.astype(F32) for p in split3(points * (2 * UNIT)))
    out[:, 0:128] = jnp.concatenate([p1, p1, p1, p2], axis=0).T.astype(BF)
    out[:, 128:256] = jnp.concatenate([p2, p3, still_terms(term, shift)], axis=0).T.astype(BF)


def still_terms(term, shift):
    n = term.shape[1]
    parts = [t.astype(F32) for t in split3(term)] + [jnp.ones((3, n), F32)]
    if shift is not None:
        parts += [t.astype(F32) for t in split3(shift)]
    return jnp.concatenate(parts + [jnp.zeros((64 - sum(p.shape[0] for p in parts), n), F32)], axis=0)


def build_moving(points, term, out):
    n = points.shape[1]
    p1, p2, p3 = split3(points)
    t1, t2, t3 = (t.astype(F32) for t in split3(term))
    for row, part in enumerate((p1, p2, p3, p1, p2, p1)):
        out[32 * row : 32 * row + 32, :] = part
    ones, zeros = jnp.ones((3, n), F32), jnp.zeros((7, n), F32)
    out[192:208, :] = jnp.concatenate([ones, t1, t2, t3, ones, zeros], axis=0).astype(BF)


def tree(op, items):
    items = list(items)
    while len(items) > 1:
        items = [op(a, b) for a, b in zip(items[::2], items[1::2])] + items[len(items) & ~1 :]
    return items[0]


def lanes(block):
    return jnp.concatenate([block[k : k + 1, :] for k in range(block.shape[0])], axis=1)


def rows(line):
    return jnp.concatenate([line[:, k : k + 128] for k in range(0, line.shape[1], 128)], axis=0)


def sweep(steps, make, multiply, process):
    make(0, 0)
    multiply(0)
    make(1, 1)

    def pair(t, carry):
        multiply(1)
        make(lax.rem(2 * t + 2, steps), 0)
        process(2 * t, 0)
        multiply(0)
        make(lax.rem(2 * t + 3, steps), 1)
        process(2 * t + 1, 1)
        return carry

    lax.fori_loop(0, steps // 2, pair, 0)


def row_first_kernel(tile, x_ref, y_ref, out, still, moving, scores, peak, total):
    count = x_ref.shape[1]
    steps = y_ref.shape[1] // tile
    x = x_ref[...]
    norm = -UNIT * square_norm(x)
    build_still(x, norm, still)
    moving[:, 208:DEPTH, :] = jnp.zeros((2, DEPTH - 208, tile), BF)
    peak[...] = jnp.zeros(peak.shape, F32)
    total[...] = jnp.zeros(total.shape, F32)

    def make(t, slot):
        y = y_ref[:, pl.ds(pl.multiple_of(t * tile, tile), tile)]
        build_moving(y, -UNIT * square_norm(y), moving.at[slot])

    def multiply(slot):
        scores[slot] = jnp.dot(still[...], moving[slot], preferred_element_type=F32)

    make(0, 0)
    sample = jnp.dot(still[...], moving[0, :, 0:256], preferred_element_type=F32)
    base = jnp.max(jnp.maximum(sample[:, 0:128], sample[:, 128:256]).T, axis=0, keepdims=True)
    _, p2, p3 = split3(x * (2 * UNIT))
    terms = still_terms(norm, -base)
    still[:, 128:256] = jnp.concatenate([p2.astype(F32), p3.astype(F32), terms], axis=0).T.astype(BF)

    def process(t, slot):
        for r in range(0, count, 8):
            e = [jnp.exp2(scores[slot, r : r + 8, k : k + 128]) for k in range(0, tile, 128)]
            total[r : r + 8, :] += tree(jnp.add, e)

    sweep(steps, make, multiply, process)

    @pl.when(jnp.max(total[...]) > 1e34)
    def _():
        peak[...] = jnp.full(peak.shape, -1e30, F32)
        total[...] = jnp.zeros(total.shape, F32)

        def step(t, carry):
            make(t, 0)
            multiply(0)
            for r in range(0, count, 8):
                s = [scores[0, r : r + 8, k : k + 128] for k in range(0, tile, 128)]
                old = peak[r : r + 8, :]
                new = jnp.maximum(old, tree(jnp.maximum, s))
                part = tree(jnp.add, [jnp.exp2(a - new) for a in s])
                total[r : r + 8, :] = total[r : r + 8, :] * jnp.exp2(old - new) + part
                peak[r : r + 8, :] = new
            return carry

        lax.fori_loop(0, steps, step, 0)

    peaks = peak[...].T
    top = jnp.max(peaks, axis=0, keepdims=True)
    whole = jnp.sum(total[...].T * jnp.exp2(peaks - top), axis=0, keepdims=True)
    pair = jnp.concatenate([rows(top + base), rows(whole)], axis=0)
    for s in range(out.shape[0]):
        out[s] = pair


def row_first(x, y, copies):
    tile, count = 1024, x.shape[1]
    return pl.pallas_call(
        functools.partial(row_first_kernel, tile),
        out_shape=jax.ShapeDtypeStruct((copies, 8, 128), F32),
        scratch_shapes=[
            pltpu.VMEM((count, DEPTH), BF),
            pltpu.VMEM((2, DEPTH, tile), BF),
            pltpu.VMEM((2, count, tile), F32),
            pltpu.VMEM((count, 128), F32),
            pltpu.VMEM((count, 128), F32),
        ],
        compiler_params=params(),
        name="row_first",
    )(x, y)


def col_first_kernel(tile, log_b, at, x0, x1, x2, x3, parts, y_ref, out, dual_out, still, moving, scores, found):
    count = x0.shape[1]
    half = found.shape[0] // 2
    for k, x_ref in enumerate((x0, x1, x2, x3)):
        row = (at[0] + 4 - k) % 4
        pieces = [parts[4 * s + row] for s in range(4)]
        top = tree(jnp.maximum, [p[0:4] for p in pieces])
        whole = tree(jnp.add, [p[4:8] * jnp.exp2(p[0:4] - top) for p in pieces])
        dual = -(top + log2(whole) + log_b)
        dual_out[4 * k : 4 * k + 4, :] = dual
        x = x_ref[...]
        build_still(x, lanes(dual) - UNIT * square_norm(x), still.at[pl.ds(count * k, count)])
    moving[:, 208:DEPTH, :] = jnp.zeros((2, DEPTH - 208, tile), BF)

    def make(t, slot):
        y = y_ref[:, pl.ds(pl.multiple_of(t * tile, tile), tile)]
        build_moving(y, -UNIT * square_norm(y), moving.at[slot])

    def multiply(slot):
        scores[slot] = jnp.dot(still[...], moving[slot], preferred_element_type=F32)

    def process(t, slot):
        for k in range(0, tile, 128):
            column = slice(k, k + 128)
            total = [jnp.exp2(scores[slot, 8 * q : 8 * q + 8, column]) for q in range(8)]
            for r in range(64, 4 * count, 64):
                total = [a + jnp.exp2(scores[slot, r + 8 * q : r + 8 * q + 8, column]) for q, a in enumerate(total)]
            found[pl.ds(half + 2 * t + k // 128, 1), :] = jnp.sum(tree(jnp.add, total), axis=0, keepdims=True)

    found[0:half, :] = jnp.zeros((half, 128), F32)
    steps = y_ref.shape[1] // tile
    sweep(steps, make, multiply, process)

    @pl.when(jnp.min(found[half:, :]) < 1e-25)
    def _():
        def step(t, carry):
            make(t, 0)
            multiply(0)
            for k in range(0, tile, 128):
                peak = jnp.full((8, 128), -1e30, F32)
                total = jnp.zeros((8, 128), F32)
                for r in range(0, 4 * count, 128):
                    s = [scores[0, r + q : r + q + 8, k : k + 128] for q in range(0, 128, 8)]
                    new = jnp.maximum(peak, tree(jnp.maximum, s))
                    total = total * jnp.exp2(peak - new) + tree(jnp.add, [jnp.exp2(a - new) for a in s])
                    peak = new
                best = jnp.max(peak, axis=0, keepdims=True)
                found[pl.ds(2 * t + k // 128, 1), :] = best
                whole = jnp.sum(total * jnp.exp2(peak - best), axis=0, keepdims=True)
                found[pl.ds(half + 2 * t + k // 128, 1), :] = whole
            return carry

        lax.fori_loop(0, steps, step, 0)

    for s in range(out.shape[0]):
        out[s] = found[...]


def at_start(shape):
    return pl.BlockSpec(shape, lambda i, at: (0,) * len(shape))


def col_first(at, blocks, parts, y, log_b, copies):
    tile, count = 256, blocks[0].shape[1]
    width = y.shape[1] // 4
    lines = width // 64
    return pl.pallas_call(
        functools.partial(col_first_kernel, tile, log_b),
        out_shape=(
            jax.ShapeDtypeStruct((copies, lines, 128), F32),
            jax.ShapeDtypeStruct((16, 128), F32),
        ),
        grid_spec=pltpu.PrefetchScalarGridSpec(
            num_scalar_prefetch=1,
            grid=(1,),
            in_specs=[at_start(b.shape) for b in blocks]
            + [at_start(parts.shape), pl.BlockSpec((32, width), lambda i, at: (0, at[0]))],
            out_specs=(at_start((copies, lines, 128)), at_start((16, 128))),
            scratch_shapes=[
                pltpu.VMEM((4 * count, DEPTH), BF),
                pltpu.VMEM((2, DEPTH, tile), BF),
                pltpu.VMEM((2, 4 * count, tile), F32),
                pltpu.VMEM((lines, 128), F32),
            ],
        ),
        compiler_params=params(),
        name="col_first",
    )(at, *blocks, parts, y)


def row_second_kernel(
    tile, log_a, log_b, at, x0, x1, x2, x3, f_ref, parts, y_ref, out, own, every, still, moving, scores, total, dual
):
    count = x0.shape[1]
    half = parts.shape[1] // 2
    top = tree(jnp.maximum, [parts[s, 0:half] for s in range(parts.shape[0])])
    whole = tree(jnp.add, [parts[s, half:] * jnp.exp2(parts[s, 0:half] - top) for s in range(parts.shape[0])])
    g = -(top + log2(whole) + log_a)
    every[...] = g
    for t in range(half // 2):
        dual[t] = g[2 * t : 2 * t + 2]
    own[...] = jnp.concatenate([dual[2 * at[1]], dual[2 * at[1] + 1]], axis=0)
    for k, x_ref in enumerate((x0, x1, x2, x3)):
        x = x_ref[...]
        f = lanes(f_ref[4 * k : 4 * k + 4])
        build_still(x, f - UNIT * square_norm(x), still.at[pl.ds(count * k, count)])
    moving[:, 208:DEPTH, :] = jnp.zeros((2, DEPTH - 208, tile), BF)
    total[...] = jnp.zeros(total.shape, F32)

    def make(t, slot):
        y = y_ref[:, pl.ds(pl.multiple_of(t * tile, tile), tile)]
        build_moving(y, lanes(dual[t]) + log_b - UNIT * square_norm(y), moving.at[slot])

    def multiply(slot):
        scores[slot] = jnp.dot(still[...], moving[slot], preferred_element_type=F32)

    def process(t, slot):
        for r in range(0, 4 * count, 8):
            e = [jnp.exp2(scores[slot, r : r + 8, k : k + 128]) for k in range(0, tile, 128)]
            total[r : r + 8, :] += tree(jnp.add, e)

    sweep(y_ref.shape[1] // tile, make, multiply, process)
    for k in range(4):
        line = jnp.sum(total[count * k : count * k + count, :].T, axis=0, keepdims=True)
        row = (at[0] + 4 - k) % 4
        for s in range(out.shape[0]):
            out[s, row] = rows(line)


def row_second(at, blocks, f, parts, y, log_a, log_b, copies):
    tile, count = 256, blocks[0].shape[1]
    width = y.shape[1] // 4
    return pl.pallas_call(
        functools.partial(row_second_kernel, tile, log_a, log_b),
        out_shape=(
            jax.ShapeDtypeStruct((copies, 4, 4, 128), F32),
            jax.ShapeDtypeStruct((4, 128), F32),
            jax.ShapeDtypeStruct((width // 128, 128), F32),
        ),
        grid_spec=pltpu.PrefetchScalarGridSpec(
            num_scalar_prefetch=1,
            grid=(1,),
            in_specs=[at_start(b.shape) for b in blocks]
            + [at_start(f.shape), at_start(parts.shape), pl.BlockSpec((32, width), lambda i, at: (0, at[0]))],
            out_specs=(at_start((copies, 4, 4, 128)), at_start((4, 128)), at_start((width // 128, 128))),
            scratch_shapes=[
                pltpu.VMEM((4 * count, DEPTH), BF),
                pltpu.VMEM((2, DEPTH, tile), BF),
                pltpu.VMEM((2, 4 * count, tile), F32),
                pltpu.VMEM((4 * count, 128), F32),
                pltpu.VMEM((width // tile, 2, 128), F32),
            ],
        ),
        compiler_params=params(),
        name="row_second",
    )(at, *blocks, f, parts, y)


def col_second_kernel(
    tile, log_a, at, x0, x1, x2, x3, f_ref, parts, y_ref, g_ref, out, own, still, moving, scores, weights, values, dual
):
    count = x0.shape[1]
    half = 4 * count
    for k, x_ref in enumerate((x0, x1, x2, x3)):
        row = (at[0] + 4 - k) % 4
        whole = tree(jnp.add, [parts[s, row] for s in range(parts.shape[0])])
        f = f_ref[4 * k : 4 * k + 4, :] - log2(whole)
        if k == 0:
            own[...] = f * (1.0 / UNIT)
        x = x_ref[...]
        build_still(x, lanes(f) - UNIT * square_norm(x), still.at[pl.ds(count * k, count)])
        for part, piece in enumerate(split3(x)):
            values[32 * part : 32 * part + 32, count * k : count * k + count] = piece
            values[32 * part : 32 * part + 32, half + count * k : half + count * k + count] = piece
    values[96:112, :] = jnp.ones((16, 2 * half), BF)
    moving[:, 208:DEPTH, :] = jnp.zeros((2, DEPTH - 208, tile), BF)
    weights[1] = jnp.zeros((2 * half, tile), BF)
    out[:, 128:136, :] = jnp.zeros((out.shape[0], 8, 128), F32)
    for t in range(dual.shape[0]):
        dual[t] = g_ref[2 * t : 2 * t + 2, :]

    def make(t, slot):
        y = y_ref[:, pl.ds(pl.multiple_of(t * tile, tile), tile)]
        build_moving(y, lanes(dual[t]) + log_a - UNIT * square_norm(y), moving.at[slot])

    def multiply(slot):
        scores[slot] = jnp.dot(still[...], moving[slot], preferred_element_type=F32)

    def weigh(slot):
        for r in range(0, half, 16):
            for k in range(0, tile, 128):
                e = jnp.exp2(scores[slot, r : r + 16, k : k + 128])
                high = e.astype(BF)
                weights[slot, r : r + 16, k : k + 128] = high
                weights[slot, half + r : half + r + 16, k : k + 128] = (e - high.astype(F32)).astype(BF)

    def gather(block, slot):
        sums = jnp.dot(values[...], weights[slot], preferred_element_type=F32)
        moment = sums[0:32] + sums[32:64] + sums[64:96]
        for h in range(2):
            k = 2 * slot + h
            out[block, 32 * k : 32 * k + 32, :] = moment[:, 128 * h : 128 * h + 128]
            out[block, 128 + k : 129 + k, :] = sums[96:97, 128 * h : 128 * h + 128]

    steps = y_ref.shape[1] // tile
    make(0, 0)
    multiply(0)
    make(1, 1)

    def pair(t, carry):
        multiply(1)
        make(lax.rem(2 * t + 2, steps), 0)
        gather(lax.rem(t + steps // 2 - 1, steps // 2), 1)
        weigh(0)
        multiply(0)
        make(lax.rem(2 * t + 3, steps), 1)
        gather(t, 0)
        weigh(1)
        return carry

    lax.fori_loop(0, steps // 2, pair, 0)
    gather(steps // 2 - 1, 1)


def col_second(at, blocks, f, parts, y, g, log_a):
    tile, count = 256, blocks[0].shape[1]
    width = y.shape[1] // 4
    return pl.pallas_call(
        functools.partial(col_second_kernel, tile, log_a),
        out_shape=(
            jax.ShapeDtypeStruct((width // 512, 136, 128), F32),
            jax.ShapeDtypeStruct((4, 128), F32),
        ),
        grid_spec=pltpu.PrefetchScalarGridSpec(
            num_scalar_prefetch=1,
            grid=(1,),
            in_specs=[at_start(b.shape) for b in blocks]
            + [at_start(f.shape), at_start(parts.shape), pl.BlockSpec((32, width), lambda i, at: (0, at[0]))]
            + [at_start(g.shape)],
            out_specs=(at_start((width // 512, 136, 128)), at_start((4, 128))),
            scratch_shapes=[
                pltpu.VMEM((4 * count, DEPTH), BF),
                pltpu.VMEM((2, DEPTH, tile), BF),
                pltpu.VMEM((2, 4 * count, tile), F32),
                pltpu.VMEM((2, 8 * count, tile), BF),
                pltpu.VMEM((112, 8 * count), BF),
                pltpu.VMEM((width // tile, 2, 128), F32),
            ],
        ),
        compiler_params=params(),
        name="col_second",
    )(at, *blocks, f, parts, y, g)


def finish_kernel(parts, g_ref, out):
    sums = tree(jnp.add, [parts[s] for s in range(parts.shape[0])])
    for k in range(4):
        out[32 * k : 32 * k + 32, :] = sums[32 * k : 32 * k + 32] / sums[128 + k : 129 + k]
    dual = (g_ref[...] - log2(sums[128:132])) * (1.0 / UNIT)
    out[128:136, :] = jnp.concatenate([dual, dual], axis=0)


def finish(parts, g):
    return pl.pallas_call(
        finish_kernel,
        out_shape=jax.ShapeDtypeStruct((136, 128), F32),
        compiler_params=params(),
        name="finish",
    )(parts, g)


TURNS = (0, 1, 3, 2)


def place_kernel(turns, at, *refs):
    mapped, dual = refs[-2:]
    y, z, core = at[0], at[1] // 2, at[1] % 2
    for n, ref in enumerate(refs[:-2]):
        turn, owner = turns[n // 2], core if n % 2 == 0 else 1 - core
        for b in range(4):
            row = jnp.where(owner == 0, y - TURNS[b], y - turn) & 3
            column = jnp.where(owner == 0, z - turn, z - TURNS[b]) & 3
            spot = row * 8 + column * 2 + owner
            for k in range(4):
                where = pl.ds(pl.multiple_of(512 * spot + 128 * k, 128), 128)
                mapped[:, where] = ref[b, 32 * k : 32 * k + 32, :]
            dual[spot] = ref[b, 128:132, :]


def place(at, pieces, turns):
    return pl.pallas_call(
        functools.partial(place_kernel, turns),
        out_shape=(jax.ShapeDtypeStruct((32, 16384), F32), jax.ShapeDtypeStruct((32, 4, 128), F32)),
        grid_spec=pltpu.PrefetchScalarGridSpec(
            num_scalar_prefetch=1,
            grid=(1,),
            in_specs=[at_start(piece.shape) for piece in pieces],
            out_specs=(at_start((32, 16384)), at_start((32, 4, 128))),
        ),
        compiler_params=params(),
        name="place",
    )(at, *pieces)


def turned(block, turn, first):
    pairs = []
    for y in range(4):
        for z in range(4):
            for core in range(2):
                along_y = (core == 0) == first
                to = ((y + turn) % 4, z) if along_y else (y, (z + turn) % 4)
                pairs.append((8 * y + 2 * z + core, 8 * to[0] + 2 * to[1] + core))
    return lax.ppermute(block, ("y", "z", "core"), pairs)


def publish(at, block):
    line = jnp.stack([block] + [turned(block, turn, True) for turn in TURNS[1:]])
    turns = (0, 2, 1, 3)
    pieces = [line] + [turned(line, turn, False) for turn in turns[1:]]
    others = [lax.ppermute(piece, "core", [(0, 1), (1, 0)]) for piece in pieces]
    return place(at, [p for pair in zip(pieces, others) for p in pair], turns)


def spread(copies, axes):
    return lax.all_to_all(copies, axes, 0, 0)


def body(x, y):
    log_a = -math.log2(x.shape[1] * 32)
    log_b = -math.log2(y.shape[1] * 4)
    place = lax.axis_index("y"), lax.axis_index(("z", "core"))
    at = jnp.stack(place).astype(jnp.int32)
    blocks = [x] + [lax.ppermute(x, "y", [(i, (i + k) % 4) for i in range(4)]) for k in (1, 2, 3)]

    first = spread(row_first(x, y, 16), ("tgt", "y"))
    partial, f1 = col_first(at, blocks, first, y, log_b, 8)
    partial = spread(partial, ("z", "core"))
    second, own_g, g1 = row_second(at, blocks, f1, partial, y, log_a, log_b, 16)
    sums, source_dual = col_second(at, blocks, f1, spread(second, ("tgt", "y")), y, g1, log_a)
    mapped, target_dual = publish(at, finish(spread(sums, ("z", "core")), own_g))
    return source_dual.reshape(-1), target_dual.reshape(-1), mapped


def solution(mesh):
    fine = Mesh(mesh.devices.reshape(4, 4, 2, 4), ("y", "z", "core", "tgt"))
    sources = ("y", "z", "core")
    return jax.shard_map(
        body,
        mesh=fine,
        in_specs=(P(None, sources), P(None, "tgt")),
        out_specs=(P(sources), P("tgt"), P(None, "tgt")),
        check_vma=False,
    )
```

```python
import functools
import math

import jax
import jax.numpy as jnp
from jax import lax
from jax.experimental import pallas as pl
from jax.experimental.pallas import tpu as pltpu
from jax.sharding import Mesh
from jax.sharding import PartitionSpec as P

EPSILON = 0.5
LOG2E = 1.4426950408889634
UNIT = LOG2E / EPSILON
BF = jnp.bfloat16
F32 = jnp.float32
DEPTH = 256
VMEM_LIMIT = 56 * 2**20


def params():
    return pltpu.CompilerParams(vmem_limit_bytes=VMEM_LIMIT)


def log2(a):
    return jnp.log(a) * LOG2E


def split3(a):
    a1 = a.astype(BF)
    rest = a - a1.astype(F32)
    a2 = rest.astype(BF)
    rest = rest - a2.astype(F32)
    return a1, a2, rest.astype(BF)


def square_norm(points):
    return jnp.sum(points * points, axis=0, keepdims=True)


def build_still(points, term, out, shift=None):
    n = points.shape[1]
    p1, p2, p3 = (p.astype(F32) for p in split3(points * (2 * UNIT)))
    out[:, 0:128] = jnp.concatenate([p1, p1, p1, p2], axis=0).T.astype(BF)
    out[:, 128:256] = jnp.concatenate([p2, p3, still_terms(term, shift)], axis=0).T.astype(BF)


def still_terms(term, shift):
    n = term.shape[1]
    parts = [t.astype(F32) for t in split3(term)] + [jnp.ones((3, n), F32)]
    if shift is not None:
        parts += [t.astype(F32) for t in split3(shift)]
    return jnp.concatenate(parts + [jnp.zeros((64 - sum(p.shape[0] for p in parts), n), F32)], axis=0)


def build_moving(points, term, out):
    n = points.shape[1]
    p1, p2, p3 = split3(points)
    t1, t2, t3 = (t.astype(F32) for t in split3(term))
    for row, part in enumerate((p1, p2, p3, p1, p2, p1)):
        out[32 * row : 32 * row + 32, :] = part
    ones, zeros = jnp.ones((3, n), F32), jnp.zeros((7, n), F32)
    out[192:208, :] = jnp.concatenate([ones, t1, t2, t3, ones, zeros], axis=0).astype(BF)


def quarter(y_ref, at, t, tile):
    start = at[0] * (y_ref.shape[1] // 4) + t * tile
    return y_ref[:, pl.ds(pl.multiple_of(start, tile), tile)]


def tree(op, items):
    items = list(items)
    while len(items) > 1:
        items = [op(a, b) for a, b in zip(items[::2], items[1::2])] + items[len(items) & ~1 :]
    return items[0]


def lanes(block):
    return jnp.concatenate([block[k : k + 1, :] for k in range(block.shape[0])], axis=1)


def rows(line):
    return jnp.concatenate([line[:, k : k + 128] for k in range(0, line.shape[1], 128)], axis=0)


def sweep(steps, make, multiply, process):
    make(0, 0)
    multiply(0)
    make(1, 1)

    def pair(t, carry):
        multiply(1)
        make(lax.rem(2 * t + 2, steps), 0)
        process(2 * t, 0)
        multiply(0)
        make(lax.rem(2 * t + 3, steps), 1)
        process(2 * t + 1, 1)
        return carry

    lax.fori_loop(0, steps // 2, pair, 0)


def near(arrays):
    return [pltpu.with_memory_space_constraint(a, pltpu.VMEM) for a in arrays]


def whole(count):
    return [pl.BlockSpec(memory_space=pltpu.VMEM)] * count


def kept(*shapes):
    return tuple(pltpu.VMEM(shape, F32) for shape in shapes)


def row_first_kernel(tile, x_ref, y_ref, out, still, moving, scores, peak, total):
    count = x_ref.shape[1]
    steps = y_ref.shape[1] // tile
    x = x_ref[...]
    norm = -UNIT * square_norm(x)
    build_still(x, norm, still)
    moving[:, 208:DEPTH, :] = jnp.zeros((2, DEPTH - 208, tile), BF)
    peak[...] = jnp.zeros(peak.shape, F32)
    total[...] = jnp.zeros(total.shape, F32)

    def make(t, slot):
        y = y_ref[:, pl.ds(pl.multiple_of(t * tile, tile), tile)]
        build_moving(y, -UNIT * square_norm(y), moving.at[slot])

    def multiply(slot):
        scores[slot] = jnp.dot(still[...], moving[slot], preferred_element_type=F32)

    make(0, 0)
    sample = jnp.dot(still[...], moving[0, :, 0:256], preferred_element_type=F32)
    base = jnp.max(jnp.maximum(sample[:, 0:128], sample[:, 128:256]).T, axis=0, keepdims=True)
    _, p2, p3 = split3(x * (2 * UNIT))
    terms = still_terms(norm, -base)
    still[:, 128:256] = jnp.concatenate([p2.astype(F32), p3.astype(F32), terms], axis=0).T.astype(BF)

    def process(t, slot):
        for r in range(0, count, 8):
            e = [jnp.exp2(scores[slot, r : r + 8, k : k + 128]) for k in range(0, tile, 128)]
            total[r : r + 8, :] += tree(jnp.add, e)

    sweep(steps, make, multiply, process)

    @pl.when(jnp.max(total[...]) > 1e34)
    def _():
        peak[...] = jnp.full(peak.shape, -1e30, F32)
        total[...] = jnp.zeros(total.shape, F32)

        def step(t, carry):
            make(t, 0)
            multiply(0)
            for r in range(0, count, 8):
                s = [scores[0, r : r + 8, k : k + 128] for k in range(0, tile, 128)]
                old = peak[r : r + 8, :]
                new = jnp.maximum(old, tree(jnp.maximum, s))
                part = tree(jnp.add, [jnp.exp2(a - new) for a in s])
                total[r : r + 8, :] = total[r : r + 8, :] * jnp.exp2(old - new) + part
                peak[r : r + 8, :] = new
            return carry

        lax.fori_loop(0, steps, step, 0)

    peaks = peak[...].T
    top = jnp.max(peaks, axis=0, keepdims=True)
    whole = jnp.sum(total[...].T * jnp.exp2(peaks - top), axis=0, keepdims=True)
    pair = jnp.concatenate([rows(top + base), rows(whole)], axis=0)
    for s in range(out.shape[0]):
        out[s] = pair


def row_first(x, y, copies):
    tile, count = 1024, x.shape[1]
    return pl.pallas_call(
        functools.partial(row_first_kernel, tile),
        in_specs=whole(2),
        out_specs=whole(1)[0],
        out_shape=kept((copies, 8, 128))[0],
        scratch_shapes=[
            pltpu.VMEM((count, DEPTH), BF),
            pltpu.VMEM((2, DEPTH, tile), BF),
            pltpu.VMEM((2, count, tile), F32),
            pltpu.VMEM((count, 128), F32),
            pltpu.VMEM((count, 128), F32),
        ],
        compiler_params=params(),
        name="row_first",
    )(*near([x, y]))


def col_first_kernel(tile, log_b, at, x0, x1, x2, x3, parts, y_ref, out, dual_out, still, moving, scores, found):
    count = x0.shape[1]
    half = found.shape[0] // 2
    for k, x_ref in enumerate((x0, x1, x2, x3)):
        row = (at[0] + 4 - k) % 4
        pieces = [parts[4 * s + row] for s in range(4)]
        top = tree(jnp.maximum, [p[0:4] for p in pieces])
        whole = tree(jnp.add, [p[4:8] * jnp.exp2(p[0:4] - top) for p in pieces])
        dual = -(top + log2(whole) + log_b)
        dual_out[4 * k : 4 * k + 4, :] = dual
        x = x_ref[...]
        build_still(x, lanes(dual) - UNIT * square_norm(x), still.at[pl.ds(count * k, count)])
    moving[:, 208:DEPTH, :] = jnp.zeros((2, DEPTH - 208, tile), BF)

    def make(t, slot):
        y = quarter(y_ref, at, t, tile)
        build_moving(y, -UNIT * square_norm(y), moving.at[slot])

    def multiply(slot):
        scores[slot] = jnp.dot(still[...], moving[slot], preferred_element_type=F32)

    def process(t, slot):
        for k in range(0, tile, 128):
            column = slice(k, k + 128)
            total = [jnp.exp2(scores[slot, 8 * q : 8 * q + 8, column]) for q in range(8)]
            for r in range(64, 4 * count, 64):
                total = [a + jnp.exp2(scores[slot, r + 8 * q : r + 8 * q + 8, column]) for q, a in enumerate(total)]
            found[pl.ds(half + 2 * t + k // 128, 1), :] = jnp.sum(tree(jnp.add, total), axis=0, keepdims=True)

    found[0:half, :] = jnp.zeros((half, 128), F32)
    steps = y_ref.shape[1] // 4 // tile
    sweep(steps, make, multiply, process)

    @pl.when(jnp.min(found[half:, :]) < 1e-25)
    def _():
        def step(t, carry):
            make(t, 0)
            multiply(0)
            for k in range(0, tile, 128):
                peak = jnp.full((8, 128), -1e30, F32)
                total = jnp.zeros((8, 128), F32)
                for r in range(0, 4 * count, 128):
                    s = [scores[0, r + q : r + q + 8, k : k + 128] for q in range(0, 128, 8)]
                    new = jnp.maximum(peak, tree(jnp.maximum, s))
                    total = total * jnp.exp2(peak - new) + tree(jnp.add, [jnp.exp2(a - new) for a in s])
                    peak = new
                best = jnp.max(peak, axis=0, keepdims=True)
                found[pl.ds(2 * t + k // 128, 1), :] = best
                whole = jnp.sum(total * jnp.exp2(peak - best), axis=0, keepdims=True)
                found[pl.ds(half + 2 * t + k // 128, 1), :] = whole
            return carry

        lax.fori_loop(0, steps, step, 0)

    out[...] = found[...]


def at_start(shape):
    return pl.BlockSpec(shape, lambda i, at: (0,) * len(shape))


def col_first(at, blocks, parts, y, log_b):
    tile, count = 256, blocks[0].shape[1]
    width = y.shape[1] // 4
    lines = width // 64
    return pl.pallas_call(
        functools.partial(col_first_kernel, tile, log_b),
        out_shape=kept((lines, 128), (16, 128)),
        grid_spec=pltpu.PrefetchScalarGridSpec(
            num_scalar_prefetch=1,
            grid=(1,),
            in_specs=whole(6),
            out_specs=whole(2),
            scratch_shapes=[
                pltpu.VMEM((4 * count, DEPTH), BF),
                pltpu.VMEM((2, DEPTH, tile), BF),
                pltpu.VMEM((2, 4 * count, tile), F32),
                pltpu.VMEM((lines, 128), F32),
            ],
        ),
        compiler_params=params(),
        name="col_first",
    )(at, *near([*blocks, parts, y]))


def row_second_kernel(
    tile, log_a, log_b, at, x0, x1, x2, x3, f_ref, y_ref, p0, p1, p2, p3, p4, p5, p6, p7, *rest
):
    count = x0.shape[1]
    out, own, every, still, moving, scores, total, dual = rest
    parts = (p0, p1, p2, p3, p4, p5, p6, p7)
    half = p0.shape[0] // 2
    top = tree(jnp.maximum, [p[0:half] for p in parts])
    whole = tree(jnp.add, [p[half:] * jnp.exp2(p[0:half] - top) for p in parts])
    g = -(top + log2(whole) + log_a)
    every[...] = g
    for t in range(half // 2):
        dual[t] = g[2 * t : 2 * t + 2]
    own[...] = jnp.concatenate([dual[2 * at[1]], dual[2 * at[1] + 1]], axis=0)
    for k, x_ref in enumerate((x0, x1, x2, x3)):
        x = x_ref[...]
        f = lanes(f_ref[4 * k : 4 * k + 4])
        build_still(x, f - UNIT * square_norm(x), still.at[pl.ds(count * k, count)])
    moving[:, 208:DEPTH, :] = jnp.zeros((2, DEPTH - 208, tile), BF)
    total[...] = jnp.zeros(total.shape, F32)

    def make(t, slot):
        y = quarter(y_ref, at, t, tile)
        build_moving(y, lanes(dual[t]) + log_b - UNIT * square_norm(y), moving.at[slot])

    def multiply(slot):
        scores[slot] = jnp.dot(still[...], moving[slot], preferred_element_type=F32)

    def process(t, slot):
        for r in range(0, 4 * count, 8):
            e = [jnp.exp2(scores[slot, r : r + 8, k : k + 128]) for k in range(0, tile, 128)]
            total[r : r + 8, :] += tree(jnp.add, e)

    sweep(y_ref.shape[1] // 4 // tile, make, multiply, process)
    for k in range(4):
        line = jnp.sum(total[count * k : count * k + count, :].T, axis=0, keepdims=True)
        row = (at[0] + 4 - k) % 4
        for s in range(out.shape[0]):
            out[s, row] = rows(line)


def row_second(at, blocks, f, parts, y, log_a, log_b, copies):
    tile, count = 256, blocks[0].shape[1]
    width = y.shape[1] // 4
    return pl.pallas_call(
        functools.partial(row_second_kernel, tile, log_a, log_b),
        out_shape=kept((copies, 4, 4, 128), (4, 128), (width // 128, 128)),
        grid_spec=pltpu.PrefetchScalarGridSpec(
            num_scalar_prefetch=1,
            grid=(1,),
            in_specs=whole(6 + len(parts)),
            out_specs=whole(3),
            scratch_shapes=[
                pltpu.VMEM((4 * count, DEPTH), BF),
                pltpu.VMEM((2, DEPTH, tile), BF),
                pltpu.VMEM((2, 4 * count, tile), F32),
                pltpu.VMEM((4 * count, 128), F32),
                pltpu.VMEM((width // tile, 2, 128), F32),
            ],
        ),
        compiler_params=params(),
        name="row_second",
    )(at, *near([*blocks, f, y, *parts]))


def col_second_kernel(
    tile, log_a, at, x0, x1, x2, x3, f_ref, parts, y_ref, g_ref, mine, other, own, still, moving, scores, weights, values, dual, out
):
    count = x0.shape[1]
    half = 4 * count
    for k, x_ref in enumerate((x0, x1, x2, x3)):
        row = (at[0] + 4 - k) % 4
        whole = tree(jnp.add, [parts[s, row] for s in range(parts.shape[0])])
        f = f_ref[4 * k : 4 * k + 4, :] - log2(whole)
        if k == 0:
            own[...] = f * (1.0 / UNIT)
        x = x_ref[...]
        build_still(x, lanes(f) - UNIT * square_norm(x), still.at[pl.ds(count * k, count)])
        for part, piece in enumerate(split3(x)):
            values[32 * part : 32 * part + 32, count * k : count * k + count] = piece
            values[32 * part : 32 * part + 32, half + count * k : half + count * k + count] = piece
    values[96:112, :] = jnp.ones((16, 2 * half), BF)
    moving[:, 208:DEPTH, :] = jnp.zeros((2, DEPTH - 208, tile), BF)
    weights[1] = jnp.zeros((2 * half, tile), BF)
    out[:, 128:136, :] = jnp.zeros((out.shape[0], 8, 128), F32)
    for t in range(dual.shape[0]):
        dual[t] = g_ref[2 * t : 2 * t + 2, :]

    def make(t, slot):
        y = quarter(y_ref, at, t, tile)
        build_moving(y, lanes(dual[t]) + log_a - UNIT * square_norm(y), moving.at[slot])

    def multiply(slot):
        scores[slot] = jnp.dot(still[...], moving[slot], preferred_element_type=F32)

    def weigh(slot):
        for r in range(0, half, 16):
            for k in range(0, tile, 128):
                e = jnp.exp2(scores[slot, r : r + 16, k : k + 128])
                high = e.astype(BF)
                weights[slot, r : r + 16, k : k + 128] = high
                weights[slot, half + r : half + r + 16, k : k + 128] = (e - high.astype(F32)).astype(BF)

    def gather(block, slot):
        sums = jnp.dot(values[...], weights[slot], preferred_element_type=F32)
        moment = sums[0:32] + sums[32:64] + sums[64:96]
        for h in range(2):
            k = 2 * slot + h
            out[block, 32 * k : 32 * k + 32, :] = moment[:, 128 * h : 128 * h + 128]
            out[block, 128 + k : 129 + k, :] = sums[96:97, 128 * h : 128 * h + 128]

    steps = y_ref.shape[1] // 4 // tile
    make(0, 0)
    multiply(0)
    make(1, 1)

    def pair(t, carry):
        multiply(1)
        make(lax.rem(2 * t + 2, steps), 0)
        gather(lax.rem(t + steps // 2 - 1, steps // 2), 1)
        weigh(0)
        multiply(0)
        make(lax.rem(2 * t + 3, steps), 1)
        gather(t, 0)
        weigh(1)
        return carry

    lax.fori_loop(0, steps // 2, pair, 0)
    gather(steps // 2 - 1, 1)
    core = at[1] % 2
    for z in range(mine.shape[0]):
        mine[z] = out[2 * z + core]
        other[z] = out[2 * z + 1 - core]


def col_second(at, blocks, f, parts, y, g, log_a):
    tile, count = 256, blocks[0].shape[1]
    width = y.shape[1] // 4
    return pl.pallas_call(
        functools.partial(col_second_kernel, tile, log_a),
        out_shape=kept(*((width // 1024, 136, 128),) * 2) + (jax.ShapeDtypeStruct((4, 128), F32),),
        grid_spec=pltpu.PrefetchScalarGridSpec(
            num_scalar_prefetch=1,
            grid=(1,),
            in_specs=whole(8),
            out_specs=whole(2) + [at_start((4, 128))],
            scratch_shapes=[
                pltpu.VMEM((4 * count, DEPTH), BF),
                pltpu.VMEM((2, DEPTH, tile), BF),
                pltpu.VMEM((2, 4 * count, tile), F32),
                pltpu.VMEM((2, 8 * count, tile), BF),
                pltpu.VMEM((112, 8 * count), BF),
                pltpu.VMEM((width // tile, 2, 128), F32),
                pltpu.VMEM((width // 512, 136, 128), F32),
            ],
        ),
        compiler_params=params(),
        name="col_second",
    )(at, *near([*blocks, f, parts, y, g]))


def merge_kernel(at, mine, other, *outs):
    for k, out in enumerate(outs):
        z = (at[1] // 2 + k) % 4
        out[...] = mine[z] + other[z]


def merge(at, mine, other):
    return pl.pallas_call(
        merge_kernel,
        out_shape=kept(*((136, 128),) * 4),
        grid_spec=pltpu.PrefetchScalarGridSpec(
            num_scalar_prefetch=1,
            grid=(1,),
            in_specs=whole(2),
            out_specs=whole(4),
        ),
        compiler_params=params(),
        name="merge",
    )(at, *near([mine, other]))


def finish_kernel(g_ref, p0, p1, p2, p3, out):
    sums = (p0[...] + p1[...]) + (p2[...] + p3[...])
    for k in range(4):
        out[32 * k : 32 * k + 32, :] = sums[32 * k : 32 * k + 32] / sums[128 + k : 129 + k]
    dual = (g_ref[...] - log2(sums[128:132])) * (1.0 / UNIT)
    out[128:136, :] = jnp.concatenate([dual, dual], axis=0)


def finish(g, parts):
    return pl.pallas_call(
        finish_kernel,
        in_specs=whole(5),
        out_specs=whole(1)[0],
        out_shape=kept((136, 128))[0],
        compiler_params=params(),
        name="finish",
    )(*near([g, *parts]))


TURNS = (0, 1, 3, 2)


def place_kernel(turns, at, *refs):
    mapped, dual = refs[-2:]
    y, z, core = at[0], at[1] // 2, at[1] % 2
    for n, ref in enumerate(refs[:-2]):
        turn, owner = turns[n // 2], core if n % 2 == 0 else 1 - core
        for b in range(4):
            row = jnp.where(owner == 0, y - TURNS[b], y - turn) & 3
            column = jnp.where(owner == 0, z - turn, z - TURNS[b]) & 3
            spot = row * 8 + column * 2 + owner
            for k in range(4):
                where = pl.ds(pl.multiple_of(512 * spot + 128 * k, 128), 128)
                mapped[:, where] = ref[b, 32 * k : 32 * k + 32, :]
            dual[spot] = ref[b, 128:132, :]


def place(at, pieces, turns):
    return pl.pallas_call(
        functools.partial(place_kernel, turns),
        out_shape=(jax.ShapeDtypeStruct((32, 16384), F32), jax.ShapeDtypeStruct((32, 4, 128), F32)),
        grid_spec=pltpu.PrefetchScalarGridSpec(
            num_scalar_prefetch=1,
            grid=(1,),
            in_specs=whole(len(pieces)),
            out_specs=(at_start((32, 16384)), at_start((32, 4, 128))),
        ),
        compiler_params=params(),
        name="place",
    )(at, *near(pieces))


def turned(block, turn, first):
    pairs = []
    for y in range(4):
        for z in range(4):
            for core in range(2):
                along_y = (core == 0) == first
                to = ((y + turn) % 4, z) if along_y else (y, (z + turn) % 4)
                pairs.append((8 * y + 2 * z + core, 8 * to[0] + 2 * to[1] + core))
    return lax.ppermute(block, ("y", "z", "core"), pairs)


def publish(at, block):
    line = jnp.stack([block] + [turned(block, turn, True) for turn in TURNS[1:]])
    turns = (0, 2, 1, 3)
    pieces = [line] + [turned(line, turn, False) for turn in turns[1:]]
    others = [lax.ppermute(piece, "core", [(0, 1), (1, 0)]) for piece in pieces]
    return place(at, [p for pair in zip(pieces, others) for p in pair], turns)


def spread(copies, axes):
    return lax.all_to_all(copies, axes, 0, 0)


def along(block, axis, turn):
    n = lax.axis_size(axis)
    return lax.ppermute(block, axis, [(i, (i + turn) % n) for i in range(n)])


def body(x, y):
    log_a = -math.log2(x.shape[1] * 32)
    log_b = -math.log2(y.shape[1] * 4)
    place = lax.axis_index("y"), lax.axis_index(("z", "core"))
    at = jnp.stack(place).astype(jnp.int32)
    first = row_first(x, y, 16)
    early, _ = lax.optimization_barrier((x, first))
    blocks = [x] + [along(early, "y", turn) for turn in (1, 2, 3)]

    partial, f1 = col_first(at, blocks, spread(first, ("tgt", "y")), y, log_b)
    partial = [partial] + [along(partial, "z", turn) for turn in (2, 1, 3)]
    partial = partial + [along(p, "core", 1) for p in partial]
    second, own_g, g1 = row_second(at, blocks, f1, partial, y, log_a, log_b, 16)
    mine, other, source_dual = col_second(at, blocks, f1, spread(second, ("tgt", "y")), y, g1, log_a)
    sums = merge(at, mine, along(other, "core", 1))
    sums = [sums[0]] + [along(sums[turn], "z", turn) for turn in (1, 2, 3)]
    mapped, target_dual = publish(at, finish(own_g, sums))
    return source_dual.reshape(-1), target_dual.reshape(-1), mapped


def solution(mesh):
    fine = Mesh(mesh.devices.reshape(4, 4, 2, 4), ("y", "z", "core", "tgt"))
    sources = ("y", "z", "core")
    return jax.shard_map(
        body,
        mesh=fine,
        in_specs=(P(None, sources), P(None, "tgt")),
        out_specs=(P(sources), P("tgt"), P(None, "tgt")),
        check_vma=False,
    )
```

```python
import functools
import math

import jax
import jax.numpy as jnp
from jax import lax
from jax.experimental import pallas as pl
from jax.experimental.pallas import tpu as pltpu
from jax.sharding import Mesh
from jax.sharding import PartitionSpec as P

EPSILON = 0.5
LOG2E = 1.4426950408889634
UNIT = LOG2E / EPSILON
BF = jnp.bfloat16
F32 = jnp.float32
DEPTH = 256
VMEM_LIMIT = 56 * 2**20


def params():
    return pltpu.CompilerParams(vmem_limit_bytes=VMEM_LIMIT)


def log2(a):
    return jnp.log(a) * LOG2E


def split3(a):
    a1 = a.astype(BF)
    rest = a - a1.astype(F32)
    a2 = rest.astype(BF)
    rest = rest - a2.astype(F32)
    return a1, a2, rest.astype(BF)


def square_norm(points):
    return jnp.sum(points * points, axis=0, keepdims=True)


def build_still(points, term, out, shift=None):
    n = points.shape[1]
    p1, p2, p3 = (p.astype(F32) for p in split3(points * (2 * UNIT)))
    out[:, 0:128] = jnp.concatenate([p1, p1, p1, p2], axis=0).T.astype(BF)
    out[:, 128:256] = jnp.concatenate([p2, p3, still_terms(term, shift)], axis=0).T.astype(BF)


def still_terms(term, shift):
    n = term.shape[1]
    parts = [t.astype(F32) for t in split3(term)] + [jnp.ones((3, n), F32)]
    if shift is not None:
        parts += [t.astype(F32) for t in split3(shift)]
    return jnp.concatenate(parts + [jnp.zeros((64 - sum(p.shape[0] for p in parts), n), F32)], axis=0)


def build_moving(points, term, out):
    n = points.shape[1]
    p1, p2, p3 = split3(points)
    t1, t2, t3 = (t.astype(F32) for t in split3(term))
    for row, part in enumerate((p1, p2, p3, p1, p2, p1)):
        out[32 * row : 32 * row + 32, :] = part
    ones, zeros = jnp.ones((3, n), F32), jnp.zeros((7, n), F32)
    out[192:208, :] = jnp.concatenate([ones, t1, t2, t3, ones, zeros], axis=0).astype(BF)


def quarter(y_ref, t, tile):
    start = lax.axis_index("y") * (y_ref.shape[1] // 4) + t * tile
    return y_ref[:, pl.ds(pl.multiple_of(start, tile), tile)]


def tree(op, items):
    items = list(items)
    while len(items) > 1:
        items = [op(a, b) for a, b in zip(items[::2], items[1::2])] + items[len(items) & ~1 :]
    return items[0]


def lanes(block):
    return jnp.concatenate([block[k : k + 1, :] for k in range(block.shape[0])], axis=1)


def rows(line):
    return jnp.concatenate([line[:, k : k + 128] for k in range(0, line.shape[1], 128)], axis=0)


def sweep(steps, make, multiply, process):
    make(0, 0)
    multiply(0)
    make(1, 1)

    def pair(t, carry):
        multiply(1)
        make(lax.rem(2 * t + 2, steps), 0)
        process(2 * t, 0)
        multiply(0)
        make(lax.rem(2 * t + 3, steps), 1)
        process(2 * t + 1, 1)
        return carry

    lax.fori_loop(0, steps // 2, pair, 0)


def near(arrays):
    return [pltpu.with_memory_space_constraint(a, pltpu.VMEM) for a in arrays]


def whole(count):
    return [pl.BlockSpec(memory_space=pltpu.VMEM)] * count


def kept(*shapes):
    return tuple(pltpu.VMEM(shape, F32) for shape in shapes)


def row_first_kernel(tile, x_far, y_far, out, y_ref, x_ref, still, moving, scores, peak, total, sem):
    count = x_ref.shape[1]
    steps = y_ref.shape[1] // tile
    ahead = 2 * tile
    get_x = pltpu.make_async_copy(x_far, x_ref, sem.at[0])
    get_first = pltpu.make_async_copy(y_far.at[:, 0:ahead], y_ref.at[:, 0:ahead], sem.at[1])
    get_rest = pltpu.make_async_copy(y_far.at[:, ahead:], y_ref.at[:, ahead:], sem.at[2])
    get_x.start()
    get_first.start()
    get_rest.start()
    get_x.wait()
    x = x_ref[...]
    norm = -UNIT * square_norm(x)
    build_still(x, norm, still)
    moving[:, 208:DEPTH, :] = jnp.zeros((2, DEPTH - 208, tile), BF)
    peak[...] = jnp.zeros(peak.shape, F32)
    total[...] = jnp.zeros(total.shape, F32)

    def make(t, slot):
        y = y_ref[:, pl.ds(pl.multiple_of(t * tile, tile), tile)]
        build_moving(y, -UNIT * square_norm(y), moving.at[slot])

    def multiply(slot):
        scores[slot] = jnp.dot(still[...], moving[slot], preferred_element_type=F32)

    get_first.wait()
    make(0, 0)
    sample = jnp.dot(still[...], moving[0, :, 0:256], preferred_element_type=F32)
    base = jnp.max(jnp.maximum(sample[:, 0:128], sample[:, 128:256]).T, axis=0, keepdims=True)
    _, p2, p3 = split3(x * (2 * UNIT))
    terms = still_terms(norm, -base)
    still[:, 128:256] = jnp.concatenate([p2.astype(F32), p3.astype(F32), terms], axis=0).T.astype(BF)

    def process(t, slot):
        for r in range(0, count, 8):
            e = [jnp.exp2(scores[slot, r : r + 8, k : k + 128]) for k in range(0, tile, 128)]
            total[r : r + 8, :] += tree(jnp.add, e)

    get_rest.wait()
    sweep(steps, make, multiply, process)

    @pl.when(jnp.max(total[...]) > 1e34)
    def _():
        peak[...] = jnp.full(peak.shape, -1e30, F32)
        total[...] = jnp.zeros(total.shape, F32)

        def step(t, carry):
            make(t, 0)
            multiply(0)
            for r in range(0, count, 8):
                s = [scores[0, r : r + 8, k : k + 128] for k in range(0, tile, 128)]
                old = peak[r : r + 8, :]
                new = jnp.maximum(old, tree(jnp.maximum, s))
                part = tree(jnp.add, [jnp.exp2(a - new) for a in s])
                total[r : r + 8, :] = total[r : r + 8, :] * jnp.exp2(old - new) + part
                peak[r : r + 8, :] = new
            return carry

        lax.fori_loop(0, steps, step, 0)

    peaks = peak[...].T
    top = jnp.max(peaks, axis=0, keepdims=True)
    whole = jnp.sum(total[...].T * jnp.exp2(peaks - top), axis=0, keepdims=True)
    pair = jnp.concatenate([rows(top + base), rows(whole)], axis=0)
    share = x_ref[pl.ds(pl.multiple_of(8 * lax.axis_index("tgt"), 8), 8), :]
    for s in range(out.shape[0]):
        out[s, 0:8] = pair
        for k in range(0, count, 128):
            out[s, 8 + k // 16 : 16 + k // 16] = share[:, k : k + 128]


def row_first(x, y, copies):
    tile, count = 1024, x.shape[1]
    return pl.pallas_call(
        functools.partial(row_first_kernel, tile),
        in_specs=[pl.BlockSpec(memory_space=pl.ANY)] * 2,
        out_specs=whole(2),
        out_shape=kept((copies, 8 + count // 16, 128), y.shape),
        scratch_shapes=[
            pltpu.VMEM(x.shape, F32),
            pltpu.VMEM((count, DEPTH), BF),
            pltpu.VMEM((2, DEPTH, tile), BF),
            pltpu.VMEM((2, count, tile), F32),
            pltpu.VMEM((count, 128), F32),
            pltpu.VMEM((count, 128), F32),
            pltpu.SemaphoreType.DMA((3,)),
        ],
        compiler_params=params(),
        name="row_first",
    )(x, y)


def col_first_kernel(tile, log_b, parts, y_ref, out, dual_out, x_out, still, moving, scores, found):
    count = x_out.shape[2]
    half = found.shape[0] // 2
    for row in range(4):
        pieces = [parts[4 * s + row] for s in range(4)]
        top = tree(jnp.maximum, [p[0:4] for p in pieces])
        total = tree(jnp.add, [p[4:8] * jnp.exp2(p[0:4] - top) for p in pieces])
        dual = -(top + log2(total) + log_b)
        dual_out[4 * row : 4 * row + 4, :] = dual
        shares = [jnp.concatenate([p[k : k + 8] for k in range(8, p.shape[0], 8)], axis=1) for p in pieces]
        x = jnp.concatenate(shares, axis=0)
        x_out[row] = x
        build_still(x, lanes(dual) - UNIT * square_norm(x), still.at[pl.ds(count * row, count)])
    moving[:, 208:DEPTH, :] = jnp.zeros((2, DEPTH - 208, tile), BF)

    def make(t, slot):
        y = quarter(y_ref, t, tile)
        build_moving(y, -UNIT * square_norm(y), moving.at[slot])

    def multiply(slot):
        scores[slot] = jnp.dot(still[...], moving[slot], preferred_element_type=F32)

    def process(t, slot):
        for k in range(0, tile, 128):
            column = slice(k, k + 128)
            total = [jnp.exp2(scores[slot, 8 * q : 8 * q + 8, column]) for q in range(8)]
            for r in range(64, 4 * count, 64):
                total = [a + jnp.exp2(scores[slot, r + 8 * q : r + 8 * q + 8, column]) for q, a in enumerate(total)]
            found[pl.ds(half + 2 * t + k // 128, 1), :] = jnp.sum(tree(jnp.add, total), axis=0, keepdims=True)

    found[0:half, :] = jnp.zeros((half, 128), F32)
    steps = y_ref.shape[1] // 4 // tile
    sweep(steps, make, multiply, process)

    @pl.when(jnp.min(found[half:, :]) < 1e-25)
    def _():
        def step(t, carry):
            make(t, 0)
            multiply(0)
            for k in range(0, tile, 128):
                peak = jnp.full((8, 128), -1e30, F32)
                total = jnp.zeros((8, 128), F32)
                for r in range(0, 4 * count, 128):
                    s = [scores[0, r + q : r + q + 8, k : k + 128] for q in range(0, 128, 8)]
                    new = jnp.maximum(peak, tree(jnp.maximum, s))
                    total = total * jnp.exp2(peak - new) + tree(jnp.add, [jnp.exp2(a - new) for a in s])
                    peak = new
                best = jnp.max(peak, axis=0, keepdims=True)
                found[pl.ds(2 * t + k // 128, 1), :] = best
                whole = jnp.sum(total * jnp.exp2(peak - best), axis=0, keepdims=True)
                found[pl.ds(half + 2 * t + k // 128, 1), :] = whole
            return carry

        lax.fori_loop(0, steps, step, 0)

    out[...] = found[...]


def col_first(parts, y, log_b, count):
    tile, width = 256, y.shape[1] // 4
    lines = width // 64
    return pl.pallas_call(
        functools.partial(col_first_kernel, tile, log_b),
        in_specs=whole(2),
        out_specs=whole(3),
        out_shape=kept((lines, 128), (16, 128), (4, 32, count)),
        scratch_shapes=[
            pltpu.VMEM((4 * count, DEPTH), BF),
            pltpu.VMEM((2, DEPTH, tile), BF),
            pltpu.VMEM((2, 4 * count, tile), F32),
            pltpu.VMEM((lines, 128), F32),
        ],
        compiler_params=params(),
        name="col_first",
    )(*near([parts, y]))


def row_second_kernel(tile, log_a, log_b, x_ref, f_ref, y_ref, *rest):
    out, own, every, still, moving, scores, total, dual = rest[8:]
    count = x_ref.shape[2]
    parts = rest[:8]
    half = parts[0].shape[0] // 2
    top = tree(jnp.maximum, [p[0:half] for p in parts])
    sums = tree(jnp.add, [p[half:] * jnp.exp2(p[0:half] - top) for p in parts])
    g = -(top + log2(sums) + log_a)
    every[...] = g
    for t in range(half // 2):
        dual[t] = g[2 * t : 2 * t + 2]
    place = 2 * lax.axis_index(("z", "core"))
    own[...] = jnp.concatenate([dual[place], dual[place + 1]], axis=0)
    for row in range(4):
        x = x_ref[row]
        f = lanes(f_ref[4 * row : 4 * row + 4])
        build_still(x, f - UNIT * square_norm(x), still.at[pl.ds(count * row, count)])
    moving[:, 208:DEPTH, :] = jnp.zeros((2, DEPTH - 208, tile), BF)
    total[...] = jnp.zeros(total.shape, F32)

    def make(t, slot):
        y = quarter(y_ref, t, tile)
        build_moving(y, lanes(dual[t]) + log_b - UNIT * square_norm(y), moving.at[slot])

    def multiply(slot):
        scores[slot] = jnp.dot(still[...], moving[slot], preferred_element_type=F32)

    def process(t, slot):
        for r in range(0, 4 * count, 8):
            e = [jnp.exp2(scores[slot, r : r + 8, k : k + 128]) for k in range(0, tile, 128)]
            total[r : r + 8, :] += tree(jnp.add, e)

    sweep(y_ref.shape[1] // 4 // tile, make, multiply, process)
    for k in range(4):
        line = jnp.sum(total[count * k : count * k + count, :].T, axis=0, keepdims=True)
        for s in range(out.shape[0]):
            out[s, k] = rows(line)


def row_second(x, f, y, parts, log_a, log_b, copies):
    tile, count, width = 256, x.shape[2], y.shape[1] // 4
    return pl.pallas_call(
        functools.partial(row_second_kernel, tile, log_a, log_b),
        in_specs=whole(3 + len(parts)),
        out_specs=whole(3),
        out_shape=kept((copies, 4, 4, 128), (4, 128), (width // 128, 128)),
        scratch_shapes=[
            pltpu.VMEM((4 * count, DEPTH), BF),
            pltpu.VMEM((2, DEPTH, tile), BF),
            pltpu.VMEM((2, 4 * count, tile), F32),
            pltpu.VMEM((4 * count, 128), F32),
            pltpu.VMEM((width // tile, 2, 128), F32),
        ],
        compiler_params=params(),
        name="row_second",
    )(*near([x, f, y, *parts]))


def col_second_kernel(tile, log_a, x_ref, f_ref, parts, y_ref, g_ref, mine, other, own, *rest):
    still, moving, scores, weights, values, dual, out, fresh = rest
    count = x_ref.shape[2]
    half = 4 * count
    for row in range(4):
        sums = tree(jnp.add, [parts[s, row] for s in range(parts.shape[0])])
        f = f_ref[4 * row : 4 * row + 4, :] - log2(sums)
        fresh[row] = f * (1.0 / UNIT)
        x = x_ref[row]
        here = slice(count * row, count * row + count)
        there = slice(half + count * row, half + count * row + count)
        build_still(x, lanes(f) - UNIT * square_norm(x), still.at[here])
        for part, piece in enumerate(split3(x)):
            values[32 * part : 32 * part + 32, here] = piece
            values[32 * part : 32 * part + 32, there] = piece
    own[...] = fresh[lax.axis_index("y")]
    values[96:112, :] = jnp.ones((16, 2 * half), BF)
    moving[:, 208:DEPTH, :] = jnp.zeros((2, DEPTH - 208, tile), BF)
    weights[1] = jnp.zeros((2 * half, tile), BF)
    out[:, 128:136, :] = jnp.zeros((out.shape[0], 8, 128), F32)
    for t in range(dual.shape[0]):
        dual[t] = g_ref[2 * t : 2 * t + 2, :]

    def make(t, slot):
        y = quarter(y_ref, t, tile)
        build_moving(y, lanes(dual[t]) + log_a - UNIT * square_norm(y), moving.at[slot])

    def multiply(slot):
        scores[slot] = jnp.dot(still[...], moving[slot], preferred_element_type=F32)

    def weigh(slot):
        for r in range(0, half, 16):
            for k in range(0, tile, 128):
                e = jnp.exp2(scores[slot, r : r + 16, k : k + 128])
                high = e.astype(BF)
                weights[slot, r : r + 16, k : k + 128] = high
                weights[slot, half + r : half + r + 16, k : k + 128] = (e - high.astype(F32)).astype(BF)

    def gather(block, slot):
        sums = jnp.dot(values[...], weights[slot], preferred_element_type=F32)
        moment = sums[0:32] + sums[32:64] + sums[64:96]
        for h in range(2):
            k = 2 * slot + h
            out[block, 32 * k : 32 * k + 32, :] = moment[:, 128 * h : 128 * h + 128]
            out[block, 128 + k : 129 + k, :] = sums[96:97, 128 * h : 128 * h + 128]

    steps = y_ref.shape[1] // 4 // tile
    make(0, 0)
    multiply(0)
    make(1, 1)

    def pair(t, carry):
        multiply(1)
        make(lax.rem(2 * t + 2, steps), 0)
        gather(lax.rem(t + steps // 2 - 1, steps // 2), 1)
        weigh(0)
        multiply(0)
        make(lax.rem(2 * t + 3, steps), 1)
        gather(t, 0)
        weigh(1)
        return carry

    lax.fori_loop(0, steps // 2, pair, 0)
    gather(steps // 2 - 1, 1)
    core = lax.axis_index("core")
    for z in range(mine.shape[0]):
        mine[z] = out[2 * z + core]
        other[z] = out[2 * z + 1 - core]


def col_second(x, f, parts, y, g, log_a):
    tile, count, width = 256, x.shape[2], y.shape[1] // 4
    return pl.pallas_call(
        functools.partial(col_second_kernel, tile, log_a),
        in_specs=whole(5),
        out_specs=whole(2) + [pl.BlockSpec((4, 128), lambda: (0, 0))],
        out_shape=kept(*((width // 1024, 136, 128),) * 2) + (jax.ShapeDtypeStruct((4, 128), F32),),
        scratch_shapes=[
            pltpu.VMEM((4 * count, DEPTH), BF),
            pltpu.VMEM((2, DEPTH, tile), BF),
            pltpu.VMEM((2, 4 * count, tile), F32),
            pltpu.VMEM((2, 8 * count, tile), BF),
            pltpu.VMEM((112, 8 * count), BF),
            pltpu.VMEM((width // tile, 2, 128), F32),
            pltpu.VMEM((width // 512, 136, 128), F32),
            pltpu.VMEM((4, 4, 128), F32),
        ],
        compiler_params=params(),
        name="col_second",
    )(*near([x, f, parts, y, g]))


def merge_kernel(mine, other, *outs):
    for k, out in enumerate(outs):
        z = (lax.axis_index("z") + k) & 3
        out[...] = mine[z] + other[z]


def merge(mine, other):
    return pl.pallas_call(
        merge_kernel,
        in_specs=whole(2),
        out_specs=whole(4),
        out_shape=kept(*((136, 128),) * 4),
        compiler_params=params(),
        name="merge",
    )(*near([mine, other]))


def finish_kernel(g_ref, p0, p1, p2, p3, out):
    sums = (p0[...] + p1[...]) + (p2[...] + p3[...])
    for k in range(4):
        out[32 * k : 32 * k + 32, :] = sums[32 * k : 32 * k + 32] / sums[128 + k : 129 + k]
    dual = (g_ref[...] - log2(sums[128:132])) * (1.0 / UNIT)
    out[128:136, :] = jnp.concatenate([dual, dual], axis=0)


def finish(g, parts):
    return pl.pallas_call(
        finish_kernel,
        in_specs=whole(5),
        out_specs=whole(1)[0],
        out_shape=kept((136, 128))[0],
        compiler_params=params(),
        name="finish",
    )(*near([g, *parts]))


TURNS = (0, 1, 3, 2)


def place_kernel(turns, *refs):
    mapped, dual = refs[-2:]
    y, z, core = lax.axis_index("y"), lax.axis_index("z"), lax.axis_index("core")
    for n, ref in enumerate(refs[:-2]):
        turn, owner = turns[n // 2], core if n % 2 == 0 else 1 - core
        for b in range(4):
            row = jnp.where(owner == 0, y - TURNS[b], y - turn) & 3
            column = jnp.where(owner == 0, z - turn, z - TURNS[b]) & 3
            spot = row * 8 + column * 2 + owner
            for k in range(4):
                where = pl.ds(pl.multiple_of(512 * spot + 128 * k, 128), 128)
                mapped[:, where] = ref[b, 32 * k : 32 * k + 32, :]
            dual[spot] = ref[b, 128:132, :]


def place(pieces, turns):
    return pl.pallas_call(
        functools.partial(place_kernel, turns),
        in_specs=whole(len(pieces)),
        out_shape=(jax.ShapeDtypeStruct((32, 16384), F32), jax.ShapeDtypeStruct((32, 4, 128), F32)),
        compiler_params=params(),
        name="place",
    )(*near(pieces))


def turned(block, turn, first):
    pairs = []
    for y in range(4):
        for z in range(4):
            for core in range(2):
                along_y = (core == 0) == first
                to = ((y + turn) % 4, z) if along_y else (y, (z + turn) % 4)
                pairs.append((8 * y + 2 * z + core, 8 * to[0] + 2 * to[1] + core))
    return lax.ppermute(block, ("y", "z", "core"), pairs)


def publish(block):
    line = jnp.stack([block] + [turned(block, turn, True) for turn in TURNS[1:]])
    turns = (0, 2, 1, 3)
    pieces = [line] + [turned(line, turn, False) for turn in turns[1:]]
    others = [lax.ppermute(piece, "core", [(0, 1), (1, 0)]) for piece in pieces]
    return place([p for pair in zip(pieces, others) for p in pair], turns)


def spread(copies, axes):
    return lax.all_to_all(copies, axes, 0, 0)


def along(block, axis, turn):
    n = lax.axis_size(axis)
    return lax.ppermute(block, axis, [(i, (i + turn) % n) for i in range(n)])


def body(x, y):
    log_a = -math.log2(x.shape[1] * 32)
    log_b = -math.log2(y.shape[1] * 4)
    first, near_y = row_first(x, y, 16)
    partial, f1, near_x = col_first(spread(first, ("tgt", "y")), near_y, log_b, x.shape[1])
    partial = [partial] + [along(partial, "z", turn) for turn in (2, 1, 3)]
    partial = partial + [along(p, "core", 1) for p in partial]
    second, own_g, g1 = row_second(near_x, f1, near_y, partial, log_a, log_b, 16)
    mine, other, source_dual = col_second(near_x, f1, spread(second, ("tgt", "y")), near_y, g1, log_a)
    sums = merge(mine, along(other, "core", 1))
    sums = [sums[0]] + [along(sums[turn], "z", turn) for turn in (1, 2, 3)]
    mapped, target_dual = publish(finish(own_g, sums))
    return source_dual.reshape(-1), target_dual.reshape(-1), mapped


def solution(mesh):
    fine = Mesh(mesh.devices.reshape(4, 4, 2, 4), ("y", "z", "core", "tgt"))
    sources = ("y", "z", "core")
    return jax.shard_map(
        body,
        mesh=fine,
        in_specs=(P(None, sources), P(None, "tgt")),
        out_specs=(P(sources), P("tgt"), P(None, "tgt")),
        check_vma=False,
    )
```

```python
import functools
import math

import jax
import jax.numpy as jnp
from jax import lax
from jax.experimental import pallas as pl
from jax.experimental.pallas import tpu as pltpu
from jax.sharding import Mesh
from jax.sharding import PartitionSpec as P

EPSILON = 0.5
LOG2E = 1.4426950408889634
UNIT = LOG2E / EPSILON
BF = jnp.bfloat16
F32 = jnp.float32
DEPTH = 256
VMEM_LIMIT = 56 * 2**20


def params():
    return pltpu.CompilerParams(vmem_limit_bytes=VMEM_LIMIT)


def log2(a):
    return jnp.log(a) * LOG2E


def split3(a):
    a1 = a.astype(BF)
    rest = a - a1.astype(F32)
    a2 = rest.astype(BF)
    rest = rest - a2.astype(F32)
    return a1, a2, rest.astype(BF)


def square_norm(points):
    return jnp.sum(points * points, axis=0, keepdims=True)


def build_still(points, term, out, shift=None):
    n = points.shape[1]
    p1, p2, p3 = (p.astype(F32) for p in split3(points * (2 * UNIT)))
    out[:, 0:128] = jnp.concatenate([p1, p1, p1, p2], axis=0).T.astype(BF)
    out[:, 128:256] = jnp.concatenate([p2, p3, still_terms(term, shift)], axis=0).T.astype(BF)


def still_terms(term, shift):
    n = term.shape[1]
    parts = [t.astype(F32) for t in split3(term)] + [jnp.ones((3, n), F32)]
    if shift is not None:
        parts += [t.astype(F32) for t in split3(shift)]
    return jnp.concatenate(parts + [jnp.zeros((64 - sum(p.shape[0] for p in parts), n), F32)], axis=0)


def build_moving(points, term, out):
    n = points.shape[1]
    p1, p2, p3 = split3(points)
    t1, t2, t3 = (t.astype(F32) for t in split3(term))
    for row, part in enumerate((p1, p2, p3, p1, p2, p1)):
        out[32 * row : 32 * row + 32, :] = part
    ones, zeros = jnp.ones((3, n), F32), jnp.zeros((7, n), F32)
    out[192:208, :] = jnp.concatenate([ones, t1, t2, t3, ones, zeros], axis=0).astype(BF)


def quarter(y_ref, t, tile):
    start = lax.axis_index("y") * (y_ref.shape[1] // 4) + t * tile
    return y_ref[:, pl.ds(pl.multiple_of(start, tile), tile)]


def tree(op, items):
    items = list(items)
    while len(items) > 1:
        items = [op(a, b) for a, b in zip(items[::2], items[1::2])] + items[len(items) & ~1 :]
    return items[0]


def lanes(block):
    return jnp.concatenate([block[k : k + 1, :] for k in range(block.shape[0])], axis=1)


def rows(line):
    return jnp.concatenate([line[:, k : k + 128] for k in range(0, line.shape[1], 128)], axis=0)


def sweep(steps, make, multiply, process):
    make(0, 0)
    multiply(0)
    make(1, 1)

    def pair(t, carry):
        multiply(1)
        make(lax.rem(2 * t + 2, steps), 0)
        process(2 * t, 0)
        multiply(0)
        make(lax.rem(2 * t + 3, steps), 1)
        process(2 * t + 1, 1)
        return carry

    lax.fori_loop(0, steps // 2, pair, 0)


def near(arrays):
    return [pltpu.with_memory_space_constraint(a, pltpu.VMEM) for a in arrays]


def whole(count):
    return [pl.BlockSpec(memory_space=pltpu.VMEM)] * count


def kept(*shapes):
    return tuple(pltpu.VMEM(shape, F32) for shape in shapes)


def row_first_kernel(tile, x_far, y_far, out, y_ref, x_ref, still, moving, scores, peak, total, sem):
    count = x_ref.shape[1]
    steps = y_ref.shape[1] // tile
    ahead = tile
    get_x = pltpu.make_async_copy(x_far, x_ref, sem.at[0])
    get_first = pltpu.make_async_copy(y_far.at[:, 0:ahead], y_ref.at[:, 0:ahead], sem.at[1])
    get_rest = pltpu.make_async_copy(y_far.at[:, ahead:], y_ref.at[:, ahead:], sem.at[2])
    get_x.start()
    get_first.start()
    get_rest.start()
    get_x.wait()
    x = x_ref[...]
    norm = -UNIT * square_norm(x)
    build_still(x, norm, still)
    moving[:, 208:DEPTH, :] = jnp.zeros((2, DEPTH - 208, tile), BF)
    peak[...] = jnp.zeros(peak.shape, F32)
    total[...] = jnp.zeros(total.shape, F32)

    def make(t, slot):
        y = y_ref[:, pl.ds(pl.multiple_of(t * tile, tile), tile)]
        build_moving(y, -UNIT * square_norm(y), moving.at[slot])

    def multiply(slot):
        scores[slot] = jnp.dot(still[...], moving[slot], preferred_element_type=F32)

    get_first.wait()
    make(0, 0)
    sample = jnp.dot(still[...], moving[0, :, 0:256], preferred_element_type=F32)
    base = jnp.max(jnp.maximum(sample[:, 0:128], sample[:, 128:256]).T, axis=0, keepdims=True)
    _, p2, p3 = split3(x * (2 * UNIT))
    terms = still_terms(norm, -base)
    still[:, 128:256] = jnp.concatenate([p2.astype(F32), p3.astype(F32), terms], axis=0).T.astype(BF)

    def process(t, slot):
        for r in range(0, count, 8):
            e = [jnp.exp2(scores[slot, r : r + 8, k : k + 128]) for k in range(0, tile, 128)]
            total[r : r + 8, :] += tree(jnp.add, e)

    get_rest.wait()
    sweep(steps, make, multiply, process)

    @pl.when(jnp.max(total[...]) > 1e34)
    def _():
        peak[...] = jnp.full(peak.shape, -1e30, F32)
        total[...] = jnp.zeros(total.shape, F32)

        def step(t, carry):
            make(t, 0)
            multiply(0)
            for r in range(0, count, 8):
                s = [scores[0, r : r + 8, k : k + 128] for k in range(0, tile, 128)]
                old = peak[r : r + 8, :]
                new = jnp.maximum(old, tree(jnp.maximum, s))
                part = tree(jnp.add, [jnp.exp2(a - new) for a in s])
                total[r : r + 8, :] = total[r : r + 8, :] * jnp.exp2(old - new) + part
                peak[r : r + 8, :] = new
            return carry

        lax.fori_loop(0, steps, step, 0)

    peaks = peak[...].T
    top = jnp.max(peaks, axis=0, keepdims=True)
    whole = jnp.sum(total[...].T * jnp.exp2(peaks - top), axis=0, keepdims=True)
    pair = jnp.concatenate([rows(top + base), rows(whole)], axis=0)
    share = x_ref[pl.ds(pl.multiple_of(8 * lax.axis_index("tgt"), 8), 8), :]
    for s in range(out.shape[0]):
        out[s, 0:8] = pair
        for k in range(0, count, 128):
            out[s, 8 + k // 16 : 16 + k // 16] = share[:, k : k + 128]


def row_first(x, y, copies):
    tile, count = 2048, x.shape[1]
    return pl.pallas_call(
        functools.partial(row_first_kernel, tile),
        in_specs=[pl.BlockSpec(memory_space=pl.ANY)] * 2,
        out_specs=whole(2),
        out_shape=kept((copies, 8 + count // 16, 128), y.shape),
        scratch_shapes=[
            pltpu.VMEM(x.shape, F32),
            pltpu.VMEM((count, DEPTH), BF),
            pltpu.VMEM((2, DEPTH, tile), BF),
            pltpu.VMEM((2, count, tile), F32),
            pltpu.VMEM((count, 128), F32),
            pltpu.VMEM((count, 128), F32),
            pltpu.SemaphoreType.DMA((3,)),
        ],
        compiler_params=params(),
        name="row_first",
    )(x, y)


def col_first_kernel(tile, log_b, parts, y_ref, out, dual_out, x_out, still, moving, scores, found):
    count = x_out.shape[2]
    half, group = found.shape[0] // 2, tile // 128
    for row in range(4):
        pieces = [parts[4 * s + row] for s in range(4)]
        top = tree(jnp.maximum, [p[0:4] for p in pieces])
        total = tree(jnp.add, [p[4:8] * jnp.exp2(p[0:4] - top) for p in pieces])
        dual = -(top + log2(total) + log_b)
        dual_out[4 * row : 4 * row + 4, :] = dual
        shares = [jnp.concatenate([p[k : k + 8] for k in range(8, p.shape[0], 8)], axis=1) for p in pieces]
        x = jnp.concatenate(shares, axis=0)
        x_out[row] = x
        build_still(x, lanes(dual) - UNIT * square_norm(x), still.at[pl.ds(count * row, count)])
    moving[:, 208:DEPTH, :] = jnp.zeros((2, DEPTH - 208, tile), BF)

    def make(t, slot):
        y = quarter(y_ref, t, tile)
        build_moving(y, -UNIT * square_norm(y), moving.at[slot])

    def multiply(slot):
        scores[slot] = jnp.dot(still[...], moving[slot], preferred_element_type=F32)

    def process(t, slot):
        for k in range(0, tile, 128):
            column = slice(k, k + 128)
            total = [jnp.exp2(scores[slot, 8 * q : 8 * q + 8, column]) for q in range(8)]
            for r in range(64, 4 * count, 64):
                total = [a + jnp.exp2(scores[slot, r + 8 * q : r + 8 * q + 8, column]) for q, a in enumerate(total)]
            found[pl.ds(half + group * t + k // 128, 1), :] = jnp.sum(tree(jnp.add, total), axis=0, keepdims=True)

    found[0:half, :] = jnp.zeros((half, 128), F32)
    steps = y_ref.shape[1] // 4 // tile
    sweep(steps, make, multiply, process)

    @pl.when(jnp.min(found[half:, :]) < 1e-25)
    def _():
        def step(t, carry):
            make(t, 0)
            multiply(0)
            for k in range(0, tile, 128):
                peak = jnp.full((8, 128), -1e30, F32)
                total = jnp.zeros((8, 128), F32)
                for r in range(0, 4 * count, 128):
                    s = [scores[0, r + q : r + q + 8, k : k + 128] for q in range(0, 128, 8)]
                    new = jnp.maximum(peak, tree(jnp.maximum, s))
                    total = total * jnp.exp2(peak - new) + tree(jnp.add, [jnp.exp2(a - new) for a in s])
                    peak = new
                best = jnp.max(peak, axis=0, keepdims=True)
                found[pl.ds(group * t + k // 128, 1), :] = best
                whole = jnp.sum(total * jnp.exp2(peak - best), axis=0, keepdims=True)
                found[pl.ds(half + group * t + k // 128, 1), :] = whole
            return carry

        lax.fori_loop(0, steps, step, 0)

    line = found[0:half] + log2(found[half:])
    for s in range(out.shape[0]):
        out[s] = line


def col_first(parts, y, log_b, count, copies):
    tile, width = 512, y.shape[1] // 4
    lines = width // 64
    return pl.pallas_call(
        functools.partial(col_first_kernel, tile, log_b),
        in_specs=whole(2),
        out_specs=whole(3),
        out_shape=kept((copies, lines // 2, 128), (16, 128), (4, 32, count)),
        scratch_shapes=[
            pltpu.VMEM((4 * count, DEPTH), BF),
            pltpu.VMEM((2, DEPTH, tile), BF),
            pltpu.VMEM((2, 4 * count, tile), F32),
            pltpu.VMEM((lines, 128), F32),
        ],
        compiler_params=params(),
        name="col_first",
    )(*near([parts, y]))


def row_second_kernel(tile, log_a, log_b, x_ref, f_ref, y_ref, parts, *rest):
    out, own, every, still, moving, scores, total, dual = rest
    count = x_ref.shape[2]
    half = parts.shape[1]
    logs = [parts[s] for s in range(parts.shape[0])]
    top = tree(jnp.maximum, logs)
    g = -(top + log2(tree(jnp.add, [jnp.exp2(p - top) for p in logs])) + log_a)
    every[...] = g
    for t in range(half // 4):
        dual[t] = g[4 * t : 4 * t + 4]
    own[...] = dual[lax.axis_index(("z", "core"))]
    for row in range(4):
        x = x_ref[row]
        f = lanes(f_ref[4 * row : 4 * row + 4])
        build_still(x, f - UNIT * square_norm(x), still.at[pl.ds(count * row, count)])
    moving[:, 208:DEPTH, :] = jnp.zeros((2, DEPTH - 208, tile), BF)
    total[...] = jnp.zeros(total.shape, F32)

    def make(t, slot):
        y = quarter(y_ref, t, tile)
        build_moving(y, lanes(dual[t]) + log_b - UNIT * square_norm(y), moving.at[slot])

    def multiply(slot):
        scores[slot] = jnp.dot(still[...], moving[slot], preferred_element_type=F32)

    def process(t, slot):
        for r in range(0, 4 * count, 8):
            e = [jnp.exp2(scores[slot, r : r + 8, k : k + 128]) for k in range(0, tile, 128)]
            total[r : r + 8, :] += tree(jnp.add, e)

    sweep(y_ref.shape[1] // 4 // tile, make, multiply, process)
    for k in range(4):
        line = jnp.sum(total[count * k : count * k + count, :].T, axis=0, keepdims=True)
        for s in range(out.shape[0]):
            out[s, k] = rows(line)


def row_second(x, f, y, parts, log_a, log_b, copies):
    tile, count, width = 512, x.shape[2], y.shape[1] // 4
    return pl.pallas_call(
        functools.partial(row_second_kernel, tile, log_a, log_b),
        in_specs=whole(4),
        out_specs=whole(3),
        out_shape=kept((copies, 4, 4, 128), (4, 128), (width // 128, 128)),
        scratch_shapes=[
            pltpu.VMEM((4 * count, DEPTH), BF),
            pltpu.VMEM((2, DEPTH, tile), BF),
            pltpu.VMEM((2, 4 * count, tile), F32),
            pltpu.VMEM((4 * count, 128), F32),
            pltpu.VMEM((width // tile, tile // 128, 128), F32),
        ],
        compiler_params=params(),
        name="row_second",
    )(*near([x, f, y, parts]))


def col_second_kernel(tile, log_a, x_ref, f_ref, parts, y_ref, g_ref, mine, other, own, *rest):
    still, moving, scores, weights, values, dual, out, fresh = rest
    count = x_ref.shape[2]
    half = 4 * count
    for row in range(4):
        sums = tree(jnp.add, [parts[s, row] for s in range(parts.shape[0])])
        f = f_ref[4 * row : 4 * row + 4, :] - log2(sums)
        fresh[row] = f * (1.0 / UNIT)
        x = x_ref[row]
        here = slice(count * row, count * row + count)
        there = slice(half + count * row, half + count * row + count)
        build_still(x, lanes(f) - UNIT * square_norm(x), still.at[here])
        for part, piece in enumerate(split3(x)):
            values[32 * part : 32 * part + 32, here] = piece
            values[32 * part : 32 * part + 32, there] = piece
    own[...] = fresh[lax.axis_index("y")]
    values[96:112, :] = jnp.ones((16, 2 * half), BF)
    moving[:, 208:DEPTH, :] = jnp.zeros((2, DEPTH - 208, tile), BF)
    weights[1] = jnp.zeros((2 * half, tile), BF)
    out[:, 128:136, :] = jnp.zeros((out.shape[0], 8, 128), F32)
    for t in range(dual.shape[0]):
        dual[t] = g_ref[2 * t : 2 * t + 2, :]

    def make(t, slot):
        y = quarter(y_ref, t, tile)
        build_moving(y, lanes(dual[t]) + log_a - UNIT * square_norm(y), moving.at[slot])

    def multiply(slot):
        scores[slot] = jnp.dot(still[...], moving[slot], preferred_element_type=F32)

    def weigh(slot):
        for r in range(0, half, 16):
            for k in range(0, tile, 128):
                e = jnp.exp2(scores[slot, r : r + 16, k : k + 128])
                high = e.astype(BF)
                weights[slot, r : r + 16, k : k + 128] = high
                weights[slot, half + r : half + r + 16, k : k + 128] = (e - high.astype(F32)).astype(BF)

    def gather(block, slot):
        sums = jnp.dot(values[...], weights[slot], preferred_element_type=F32)
        moment = sums[0:32] + sums[32:64] + sums[64:96]
        for h in range(2):
            k = 2 * slot + h
            out[block, 32 * k : 32 * k + 32, :] = moment[:, 128 * h : 128 * h + 128]
            out[block, 128 + k : 129 + k, :] = sums[96:97, 128 * h : 128 * h + 128]

    steps = y_ref.shape[1] // 4 // tile
    make(0, 0)
    multiply(0)
    make(1, 1)

    def pair(t, carry):
        multiply(1)
        make(lax.rem(2 * t + 2, steps), 0)
        gather(lax.rem(t + steps // 2 - 1, steps // 2), 1)
        weigh(0)
        multiply(0)
        make(lax.rem(2 * t + 3, steps), 1)
        gather(t, 0)
        weigh(1)
        return carry

    lax.fori_loop(0, steps // 2, pair, 0)
    gather(steps // 2 - 1, 1)
    core = lax.axis_index("core")
    for z in range(mine.shape[0]):
        mine[z] = out[2 * z + core]
        other[z] = out[2 * z + 1 - core]


def col_second(x, f, parts, y, g, log_a):
    tile, count, width = 256, x.shape[2], y.shape[1] // 4
    return pl.pallas_call(
        functools.partial(col_second_kernel, tile, log_a),
        in_specs=whole(5),
        out_specs=whole(2) + [pl.BlockSpec((4, 128), lambda: (0, 0))],
        out_shape=kept(*((width // 1024, 136, 128),) * 2) + (jax.ShapeDtypeStruct((4, 128), F32),),
        scratch_shapes=[
            pltpu.VMEM((4 * count, DEPTH), BF),
            pltpu.VMEM((2, DEPTH, tile), BF),
            pltpu.VMEM((2, 4 * count, tile), F32),
            pltpu.VMEM((2, 8 * count, tile), BF),
            pltpu.VMEM((112, 8 * count), BF),
            pltpu.VMEM((width // tile, 2, 128), F32),
            pltpu.VMEM((width // 512, 136, 128), F32),
            pltpu.VMEM((4, 4, 128), F32),
        ],
        compiler_params=params(),
        name="col_second",
    )(*near([x, f, parts, y, g]))


def merge_kernel(mine, other, *outs):
    for k, out in enumerate(outs):
        z = (lax.axis_index("z") + k) & 3
        out[...] = mine[z] + other[z]


def merge(mine, other):
    return pl.pallas_call(
        merge_kernel,
        in_specs=whole(2),
        out_specs=whole(4),
        out_shape=kept(*((136, 128),) * 4),
        compiler_params=params(),
        name="merge",
    )(*near([mine, other]))


def finish_kernel(g_ref, p0, p1, p2, p3, out):
    sums = (p0[...] + p1[...]) + (p2[...] + p3[...])
    for k in range(4):
        out[32 * k : 32 * k + 32, :] = sums[32 * k : 32 * k + 32] / sums[128 + k : 129 + k]
    dual = (g_ref[...] - log2(sums[128:132])) * (1.0 / UNIT)
    out[128:136, :] = jnp.concatenate([dual, dual], axis=0)


def finish(g, parts):
    return pl.pallas_call(
        finish_kernel,
        in_specs=whole(5),
        out_specs=whole(1)[0],
        out_shape=kept((136, 128))[0],
        compiler_params=params(),
        name="finish",
    )(*near([g, *parts]))


TURNS = (0, 1, 3, 2)


def place_kernel(turns, *refs):
    mapped, dual = refs[-2:]
    y, z, core = lax.axis_index("y"), lax.axis_index("z"), lax.axis_index("core")
    for n, ref in enumerate(refs[:-2]):
        turn, owner = turns[n // 2], core if n % 2 == 0 else 1 - core
        for b in range(4):
            row = jnp.where(owner == 0, y - TURNS[b], y - turn) & 3
            column = jnp.where(owner == 0, z - turn, z - TURNS[b]) & 3
            spot = row * 8 + column * 2 + owner
            for k in range(4):
                where = pl.ds(pl.multiple_of(512 * spot + 128 * k, 128), 128)
                mapped[:, where] = ref[b, 32 * k : 32 * k + 32, :]
            dual[spot] = ref[b, 128:132, :]


def place(pieces, turns):
    return pl.pallas_call(
        functools.partial(place_kernel, turns),
        in_specs=whole(len(pieces)),
        out_shape=(jax.ShapeDtypeStruct((32, 16384), F32), jax.ShapeDtypeStruct((32, 4, 128), F32)),
        compiler_params=params(),
        name="place",
    )(*near(pieces))


def turned(block, turn, first):
    pairs = []
    for y in range(4):
        for z in range(4):
            for core in range(2):
                along_y = (core == 0) == first
                to = ((y + turn) % 4, z) if along_y else (y, (z + turn) % 4)
                pairs.append((8 * y + 2 * z + core, 8 * to[0] + 2 * to[1] + core))
    return lax.ppermute(block, ("y", "z", "core"), pairs)


def publish(block):
    line = jnp.stack([block] + [turned(block, turn, True) for turn in TURNS[1:]])
    turns = (0, 2, 1, 3)
    pieces = [line] + [turned(line, turn, False) for turn in turns[1:]]
    others = [lax.ppermute(piece, "core", [(0, 1), (1, 0)]) for piece in pieces]
    return place([p for pair in zip(pieces, others) for p in pair], turns)


def spread(copies, axes):
    return lax.all_to_all(copies, axes, 0, 0)


def along(block, axis, turn):
    n = lax.axis_size(axis)
    return lax.ppermute(block, axis, [(i, (i + turn) % n) for i in range(n)])


def body(x, y):
    log_a = -math.log2(x.shape[1] * 32)
    log_b = -math.log2(y.shape[1] * 4)
    first, near_y = row_first(x, y, 16)
    partial, f1, near_x = col_first(spread(first, ("tgt", "y")), near_y, log_b, x.shape[1], 8)
    partial = spread(partial, ("z", "core"))
    second, own_g, g1 = row_second(near_x, f1, near_y, partial, log_a, log_b, 16)
    mine, other, source_dual = col_second(near_x, f1, spread(second, ("tgt", "y")), near_y, g1, log_a)
    sums = merge(mine, along(other, "core", 1))
    sums = [sums[0]] + [along(sums[turn], "z", turn) for turn in (1, 2, 3)]
    mapped, target_dual = publish(finish(own_g, sums))
    return source_dual.reshape(-1), target_dual.reshape(-1), mapped


def solution(mesh):
    fine = Mesh(mesh.devices.reshape(4, 4, 2, 4), ("y", "z", "core", "tgt"))
    sources = ("y", "z", "core")
    return jax.shard_map(
        body,
        mesh=fine,
        in_specs=(P(None, sources), P(None, "tgt")),
        out_specs=(P(sources), P("tgt"), P(None, "tgt")),
        check_vma=False,
    )
```

```python
import functools
import math

import jax
import jax.numpy as jnp
from jax import lax
from jax.experimental import pallas as pl
from jax.experimental.pallas import tpu as pltpu
from jax.sharding import Mesh
from jax.sharding import PartitionSpec as P

EPSILON = 0.5
LOG2E = 1.4426950408889634
UNIT = LOG2E / EPSILON
BF = jnp.bfloat16
F32 = jnp.float32
DEPTH = 256
VMEM_LIMIT = 56 * 2**20


def params():
    return pltpu.CompilerParams(vmem_limit_bytes=VMEM_LIMIT)


def log2(a):
    return jnp.log(a) * LOG2E


def split3(a):
    a1 = a.astype(BF)
    rest = a - a1.astype(F32)
    a2 = rest.astype(BF)
    rest = rest - a2.astype(F32)
    return a1, a2, rest.astype(BF)


def square_norm(points):
    return jnp.sum(points * points, axis=0, keepdims=True)


def build_still(points, term, out, shift=None):
    n = points.shape[1]
    p1, p2, p3 = (p.astype(F32) for p in split3(points * (2 * UNIT)))
    out[:, 0:128] = jnp.concatenate([p1, p1, p1, p2], axis=0).T.astype(BF)
    out[:, 128:256] = jnp.concatenate([p2, p3, still_terms(term, shift)], axis=0).T.astype(BF)


def still_terms(term, shift):
    n = term.shape[1]
    parts = [t.astype(F32) for t in split3(term)] + [jnp.ones((3, n), F32)]
    if shift is not None:
        parts += [t.astype(F32) for t in split3(shift)]
    return jnp.concatenate(parts + [jnp.zeros((64 - sum(p.shape[0] for p in parts), n), F32)], axis=0)


def build_moving(points, term, out):
    n = points.shape[1]
    p1, p2, p3 = split3(points)
    t1, t2, t3 = (t.astype(F32) for t in split3(term))
    for row, part in enumerate((p1, p2, p3, p1, p2, p1)):
        out[32 * row : 32 * row + 32, :] = part
    ones, zeros = jnp.ones((3, n), F32), jnp.zeros((7, n), F32)
    out[192:208, :] = jnp.concatenate([ones, t1, t2, t3, ones, zeros], axis=0).astype(BF)


def quarter(y_ref, t, tile):
    start = lax.axis_index("y") * (y_ref.shape[1] // 4) + t * tile
    return y_ref[:, pl.ds(pl.multiple_of(start, tile), tile)]


def tree(op, items):
    items = list(items)
    while len(items) > 1:
        items = [op(a, b) for a, b in zip(items[::2], items[1::2])] + items[len(items) & ~1 :]
    return items[0]


def lanes(block):
    return jnp.concatenate([block[k : k + 1, :] for k in range(block.shape[0])], axis=1)


def rows(line):
    return jnp.concatenate([line[:, k : k + 128] for k in range(0, line.shape[1], 128)], axis=0)


def sweep(steps, make, multiply, process):
    make(0, 0)
    multiply(0)
    make(1, 1)

    def pair(t, carry):
        multiply(1)
        make(lax.rem(2 * t + 2, steps), 0)
        process(2 * t, 0)
        multiply(0)
        make(lax.rem(2 * t + 3, steps), 1)
        process(2 * t + 1, 1)
        return carry

    lax.fori_loop(0, steps // 2, pair, 0)


def near(arrays):
    return [pltpu.with_memory_space_constraint(a, pltpu.VMEM) for a in arrays]


def whole(count):
    return [pl.BlockSpec(memory_space=pltpu.VMEM)] * count


def kept(*shapes):
    return tuple(pltpu.VMEM(shape, F32) for shape in shapes)


def row_first_kernel(tile, x_far, y_far, out, y_ref, x_ref, still, moving, scores, peak, total, sem):
    count = x_ref.shape[1]
    steps = y_ref.shape[1] // tile
    ahead = tile
    get_x = pltpu.make_async_copy(x_far, x_ref, sem.at[0])
    get_first = pltpu.make_async_copy(y_far.at[:, 0:ahead], y_ref.at[:, 0:ahead], sem.at[1])
    get_rest = pltpu.make_async_copy(y_far.at[:, ahead:], y_ref.at[:, ahead:], sem.at[2])
    get_x.start()
    get_first.start()
    get_rest.start()
    get_x.wait()
    x = x_ref[...]
    norm = -UNIT * square_norm(x)
    build_still(x, norm, still)
    moving[:, 208:DEPTH, :] = jnp.zeros((2, DEPTH - 208, tile), BF)
    peak[...] = jnp.zeros(peak.shape, F32)
    total[...] = jnp.zeros(total.shape, F32)

    def make(t, slot):
        y = y_ref[:, pl.ds(pl.multiple_of(t * tile, tile), tile)]
        build_moving(y, -UNIT * square_norm(y), moving.at[slot])

    def multiply(slot):
        scores[slot] = jnp.dot(still[...], moving[slot], preferred_element_type=F32)

    get_first.wait()
    make(0, 0)
    sample = jnp.dot(still[...], moving[0, :, 0:256], preferred_element_type=F32)
    base = jnp.max(jnp.maximum(sample[:, 0:128], sample[:, 128:256]).T, axis=0, keepdims=True)
    _, p2, p3 = split3(x * (2 * UNIT))
    terms = still_terms(norm, -base)
    still[:, 128:256] = jnp.concatenate([p2.astype(F32), p3.astype(F32), terms], axis=0).T.astype(BF)

    def process(t, slot):
        for r in range(0, count, 8):
            e = [jnp.exp2(scores[slot, r : r + 8, k : k + 128]) for k in range(0, tile, 128)]
            total[r : r + 8, :] += tree(jnp.add, e)

    get_rest.wait()
    sweep(steps, make, multiply, process)

    @pl.when(jnp.max(total[...]) > 1e34)
    def _():
        peak[...] = jnp.full(peak.shape, -1e30, F32)
        total[...] = jnp.zeros(total.shape, F32)

        def step(t, carry):
            make(t, 0)
            multiply(0)
            for r in range(0, count, 8):
                s = [scores[0, r : r + 8, k : k + 128] for k in range(0, tile, 128)]
                old = peak[r : r + 8, :]
                new = jnp.maximum(old, tree(jnp.maximum, s))
                part = tree(jnp.add, [jnp.exp2(a - new) for a in s])
                total[r : r + 8, :] = total[r : r + 8, :] * jnp.exp2(old - new) + part
                peak[r : r + 8, :] = new
            return carry

        lax.fori_loop(0, steps, step, 0)

    peaks = peak[...].T
    top = jnp.max(peaks, axis=0, keepdims=True)
    whole = jnp.sum(total[...].T * jnp.exp2(peaks - top), axis=0, keepdims=True)
    pair = jnp.concatenate([rows(top + base), rows(whole)], axis=0)
    share = x_ref[pl.ds(pl.multiple_of(8 * lax.axis_index("tgt"), 8), 8), :]
    for s in range(out.shape[0]):
        out[s, 0:8] = pair
        for k in range(0, count, 128):
            out[s, 8 + k // 16 : 16 + k // 16] = share[:, k : k + 128]


def row_first(x, y, copies):
    tile, count = 2048, x.shape[1]
    return pl.pallas_call(
        functools.partial(row_first_kernel, tile),
        in_specs=[pl.BlockSpec(memory_space=pl.ANY)] * 2,
        out_specs=whole(2),
        out_shape=kept((copies, 8 + count // 16, 128), y.shape),
        scratch_shapes=[
            pltpu.VMEM(x.shape, F32),
            pltpu.VMEM((count, DEPTH), BF),
            pltpu.VMEM((2, DEPTH, tile), BF),
            pltpu.VMEM((2, count, tile), F32),
            pltpu.VMEM((count, 128), F32),
            pltpu.VMEM((count, 128), F32),
            pltpu.SemaphoreType.DMA((3,)),
        ],
        compiler_params=params(),
        name="row_first",
    )(x, y)


def col_first_kernel(tile, log_b, parts, y_ref, out, dual_out, x_out, still, moving, scores, found):
    count = x_out.shape[2]
    half, group = found.shape[0] // 2, tile // 128
    for row in range(4):
        pieces = [parts[4 * s + row] for s in range(4)]
        top = tree(jnp.maximum, [p[0:4] for p in pieces])
        total = tree(jnp.add, [p[4:8] * jnp.exp2(p[0:4] - top) for p in pieces])
        dual = -(top + log2(total) + log_b)
        dual_out[4 * row : 4 * row + 4, :] = dual
        shares = [jnp.concatenate([p[k : k + 8] for k in range(8, p.shape[0], 8)], axis=1) for p in pieces]
        x = jnp.concatenate(shares, axis=0)
        x_out[row] = x
        build_still(x, lanes(dual) - UNIT * square_norm(x), still.at[pl.ds(count * row, count)])
    moving[:, 208:DEPTH, :] = jnp.zeros((2, DEPTH - 208, tile), BF)

    def make(t, slot):
        y = quarter(y_ref, t, tile)
        build_moving(y, -UNIT * square_norm(y), moving.at[slot])

    def multiply(slot):
        scores[slot] = jnp.dot(still[...], moving[slot], preferred_element_type=F32)

    def process(t, slot):
        for k in range(0, tile, 128):
            column = slice(k, k + 128)
            total = [jnp.exp2(scores[slot, 8 * q : 8 * q + 8, column]) for q in range(8)]
            for r in range(64, 4 * count, 64):
                total = [a + jnp.exp2(scores[slot, r + 8 * q : r + 8 * q + 8, column]) for q, a in enumerate(total)]
            found[pl.ds(half + group * t + k // 128, 1), :] = jnp.sum(tree(jnp.add, total), axis=0, keepdims=True)

    found[0:half, :] = jnp.zeros((half, 128), F32)
    steps = y_ref.shape[1] // 4 // tile
    sweep(steps, make, multiply, process)

    @pl.when(jnp.min(found[half:, :]) < 1e-25)
    def _():
        def step(t, carry):
            make(t, 0)
            multiply(0)
            for k in range(0, tile, 128):
                peak = jnp.full((8, 128), -1e30, F32)
                total = jnp.zeros((8, 128), F32)
                for r in range(0, 4 * count, 128):
                    s = [scores[0, r + q : r + q + 8, k : k + 128] for q in range(0, 128, 8)]
                    new = jnp.maximum(peak, tree(jnp.maximum, s))
                    total = total * jnp.exp2(peak - new) + tree(jnp.add, [jnp.exp2(a - new) for a in s])
                    peak = new
                best = jnp.max(peak, axis=0, keepdims=True)
                found[pl.ds(group * t + k // 128, 1), :] = best
                whole = jnp.sum(total * jnp.exp2(peak - best), axis=0, keepdims=True)
                found[pl.ds(half + group * t + k // 128, 1), :] = whole
            return carry

        lax.fori_loop(0, steps, step, 0)

    line = found[0:half] + log2(found[half:])
    for s in range(out.shape[0]):
        out[s] = line


def col_first(parts, y, log_b, count, copies):
    tile, width = 512, y.shape[1] // 4
    lines = width // 64
    return pl.pallas_call(
        functools.partial(col_first_kernel, tile, log_b),
        in_specs=whole(2),
        out_specs=whole(3),
        out_shape=kept((copies, lines // 2, 128), (16, 128), (4, 32, count)),
        scratch_shapes=[
            pltpu.VMEM((4 * count, DEPTH), BF),
            pltpu.VMEM((2, DEPTH, tile), BF),
            pltpu.VMEM((2, 4 * count, tile), F32),
            pltpu.VMEM((lines, 128), F32),
        ],
        compiler_params=params(),
        name="col_first",
    )(*near([parts, y]))


def row_second_kernel(tile, log_a, log_b, x_ref, f_ref, y_ref, parts, *rest):
    out, own, every, still, moving, scores, total, dual = rest
    count = x_ref.shape[2]
    half = parts.shape[1]
    logs = [parts[s] for s in range(parts.shape[0])]
    top = tree(jnp.maximum, logs)
    g = -(top + log2(tree(jnp.add, [jnp.exp2(p - top) for p in logs])) + log_a)
    every[...] = g
    for t in range(half // 4):
        dual[t] = g[4 * t : 4 * t + 4]
    own[...] = dual[lax.axis_index(("z", "core"))]
    for row in range(4):
        x = x_ref[row]
        f = lanes(f_ref[4 * row : 4 * row + 4])
        build_still(x, f - UNIT * square_norm(x), still.at[pl.ds(count * row, count)])
    moving[:, 208:DEPTH, :] = jnp.zeros((2, DEPTH - 208, tile), BF)
    total[...] = jnp.zeros(total.shape, F32)

    def make(t, slot):
        y = quarter(y_ref, t, tile)
        build_moving(y, lanes(dual[t]) + log_b - UNIT * square_norm(y), moving.at[slot])

    def multiply(slot):
        scores[slot] = jnp.dot(still[...], moving[slot], preferred_element_type=F32)

    def process(t, slot):
        for r in range(0, 4 * count, 8):
            e = [jnp.exp2(scores[slot, r : r + 8, k : k + 128]) for k in range(0, tile, 128)]
            total[r : r + 8, :] += tree(jnp.add, e)

    sweep(y_ref.shape[1] // 4 // tile, make, multiply, process)
    for k in range(4):
        line = jnp.sum(total[count * k : count * k + count, :].T, axis=0, keepdims=True)
        for s in range(out.shape[0]):
            out[s, k] = rows(line)


def row_second(x, f, y, parts, log_a, log_b, copies):
    tile, count, width = 512, x.shape[2], y.shape[1] // 4
    return pl.pallas_call(
        functools.partial(row_second_kernel, tile, log_a, log_b),
        in_specs=whole(4),
        out_specs=whole(3),
        out_shape=kept((copies, 4, 4, 128), (4, 128), (width // 128, 128)),
        scratch_shapes=[
            pltpu.VMEM((4 * count, DEPTH), BF),
            pltpu.VMEM((2, DEPTH, tile), BF),
            pltpu.VMEM((2, 4 * count, tile), F32),
            pltpu.VMEM((4 * count, 128), F32),
            pltpu.VMEM((width // tile, tile // 128, 128), F32),
        ],
        compiler_params=params(),
        name="row_second",
    )(*near([x, f, y, parts]))


def col_second_kernel(tile, log_a, x_ref, f_ref, parts, y_ref, g_ref, mine, other, own, *rest):
    still, moving, scores, weights, values, dual, out, fresh = rest
    count = x_ref.shape[2]
    half = 4 * count
    for row in range(4):
        sums = tree(jnp.add, [parts[s, row] for s in range(parts.shape[0])])
        f = f_ref[4 * row : 4 * row + 4, :] - log2(sums)
        fresh[row] = f * (1.0 / UNIT)
        x = x_ref[row]
        here = slice(count * row, count * row + count)
        there = slice(half + count * row, half + count * row + count)
        build_still(x, lanes(f) - UNIT * square_norm(x), still.at[here])
        for part, piece in enumerate(split3(x)):
            values[32 * part : 32 * part + 32, here] = piece
            values[32 * part : 32 * part + 32, there] = piece
    own[...] = fresh[lax.axis_index("y")]
    values[96:112, :] = jnp.ones((16, 2 * half), BF)
    moving[:, 208:DEPTH, :] = jnp.zeros((2, DEPTH - 208, tile), BF)
    weights[1] = jnp.zeros((2 * half, tile), BF)
    out[:, 128:136, :] = jnp.zeros((out.shape[0], 8, 128), F32)
    for t in range(dual.shape[0]):
        dual[t] = g_ref[2 * t : 2 * t + 2, :]

    def make(t, slot):
        y = quarter(y_ref, t, tile)
        build_moving(y, lanes(dual[t]) + log_a - UNIT * square_norm(y), moving.at[slot])

    def multiply(slot):
        scores[slot] = jnp.dot(still[...], moving[slot], preferred_element_type=F32)

    def weigh(slot):
        for r in range(0, half, 16):
            for k in range(0, tile, 128):
                e = jnp.exp2(scores[slot, r : r + 16, k : k + 128])
                high = e.astype(BF)
                weights[slot, r : r + 16, k : k + 128] = high
                weights[slot, half + r : half + r + 16, k : k + 128] = (e - high.astype(F32)).astype(BF)

    def gather(block, slot):
        sums = jnp.dot(values[...], weights[slot], preferred_element_type=F32)
        moment = sums[0:32] + sums[32:64] + sums[64:96]
        for h in range(2):
            k = 2 * slot + h
            out[block, 32 * k : 32 * k + 32, :] = moment[:, 128 * h : 128 * h + 128]
            out[block, 128 + k : 129 + k, :] = sums[96:97, 128 * h : 128 * h + 128]

    steps = y_ref.shape[1] // 4 // tile
    make(0, 0)
    multiply(0)
    make(1, 1)

    def pair(t, carry):
        multiply(1)
        make(lax.rem(2 * t + 2, steps), 0)
        gather(lax.rem(t + steps // 2 - 1, steps // 2), 1)
        weigh(0)
        multiply(0)
        make(lax.rem(2 * t + 3, steps), 1)
        gather(t, 0)
        weigh(1)
        return carry

    lax.fori_loop(0, steps // 2, pair, 0)
    gather(steps // 2 - 1, 1)
    core = lax.axis_index("core")
    for z in range(mine.shape[0]):
        mine[z] = out[2 * z + core]
        other[z] = out[2 * z + 1 - core]


def col_second(x, f, parts, y, g, log_a):
    tile, count, width = 256, x.shape[2], y.shape[1] // 4
    return pl.pallas_call(
        functools.partial(col_second_kernel, tile, log_a),
        in_specs=whole(5),
        out_specs=whole(2) + [pl.BlockSpec((4, 128), lambda: (0, 0))],
        out_shape=kept(*((width // 1024, 136, 128),) * 2) + (jax.ShapeDtypeStruct((4, 128), F32),),
        scratch_shapes=[
            pltpu.VMEM((4 * count, DEPTH), BF),
            pltpu.VMEM((2, DEPTH, tile), BF),
            pltpu.VMEM((2, 4 * count, tile), F32),
            pltpu.VMEM((2, 8 * count, tile), BF),
            pltpu.VMEM((112, 8 * count), BF),
            pltpu.VMEM((width // tile, 2, 128), F32),
            pltpu.VMEM((width // 512, 136, 128), F32),
            pltpu.VMEM((4, 4, 128), F32),
        ],
        compiler_params=params(),
        name="col_second",
    )(*near([x, f, parts, y, g]))


def merge_kernel(mine, other, *outs):
    for k, out in enumerate(outs):
        z = (lax.axis_index("z") + k) & 3
        out[...] = mine[z] + other[z]


def merge(mine, other):
    return pl.pallas_call(
        merge_kernel,
        in_specs=whole(2),
        out_specs=whole(4),
        out_shape=kept(*((136, 128),) * 4),
        compiler_params=params(),
        name="merge",
    )(*near([mine, other]))


def finish_kernel(g_ref, p0, p1, p2, p3, out):
    sums = (p0[...] + p1[...]) + (p2[...] + p3[...])
    for k in range(4):
        out[32 * k : 32 * k + 32, :] = sums[32 * k : 32 * k + 32] / sums[128 + k : 129 + k]
    dual = (g_ref[...] - log2(sums[128:132])) * (1.0 / UNIT)
    out[128:136, :] = jnp.concatenate([dual, dual], axis=0)


def finish(g, parts):
    return pl.pallas_call(
        finish_kernel,
        in_specs=whole(5),
        out_specs=whole(1)[0],
        out_shape=kept((136, 128))[0],
        compiler_params=params(),
        name="finish",
    )(*near([g, *parts]))


TURNS = (0, 1, 3, 2)


def place_kernel(turns, *refs):
    mapped, dual = refs[-2:]
    y, z, core = lax.axis_index("y"), lax.axis_index("z"), lax.axis_index("core")
    for n, ref in enumerate(refs[:-2]):
        turn, owner = turns[n // 2], core if n % 2 == 0 else 1 - core
        for b in range(4):
            row = jnp.where(owner == 0, y - TURNS[b], y - turn) & 3
            column = jnp.where(owner == 0, z - turn, z - TURNS[b]) & 3
            spot = row * 8 + column * 2 + owner
            for k in range(4):
                where = pl.ds(pl.multiple_of(512 * spot + 128 * k, 128), 128)
                mapped[:, where] = ref[b, 32 * k : 32 * k + 32, :]
            dual[spot] = ref[b, 128:132, :]


def place(pieces, turns):
    return pl.pallas_call(
        functools.partial(place_kernel, turns),
        in_specs=whole(len(pieces)),
        out_shape=(jax.ShapeDtypeStruct((32, 16384), F32), jax.ShapeDtypeStruct((32, 4, 128), F32)),
        compiler_params=params(),
        name="place",
    )(*near(pieces))


def turned(block, turn, first):
    pairs = []
    for y in range(4):
        for z in range(4):
            for core in range(2):
                along_y = (core == 0) == first
                to = ((y + turn) % 4, z) if along_y else (y, (z + turn) % 4)
                pairs.append((8 * y + 2 * z + core, 8 * to[0] + 2 * to[1] + core))
    return lax.ppermute(block, ("y", "z", "core"), pairs)


def publish(block):
    line = jnp.stack([block] + [turned(block, turn, True) for turn in TURNS[1:]])
    turns = (0, 2, 1, 3)
    pieces = [line] + [turned(line, turn, False) for turn in turns[1:]]
    others = [lax.ppermute(piece, "core", [(0, 1), (1, 0)]) for piece in pieces]
    return place([p for pair in zip(pieces, others) for p in pair], turns)


def spread(copies, axes):
    return lax.all_to_all(copies, axes, 0, 0)


def along(block, axis, turn):
    n = lax.axis_size(axis)
    return lax.ppermute(block, axis, [(i, (i + turn) % n) for i in range(n)])


def body(x, y):
    log_a = -math.log2(x.shape[1] * 32)
    log_b = -math.log2(y.shape[1] * 4)
    first, near_y = row_first(x, y, 16)
    partial, f1, near_x = col_first(spread(first, ("tgt", "y")), near_y, log_b, x.shape[1], 8)
    partial = spread(partial, ("z", "core"))
    second, own_g, g1 = row_second(near_x, f1, near_y, partial, log_a, log_b, 16)
    mine, other, source_dual = col_second(near_x, f1, spread(second, ("tgt", "y")), near_y, g1, log_a)
    sums = merge(mine, along(other, "core", 1))
    sums = [sums[0]] + [along(sums[turn], "z", turn) for turn in (2, 1, 3)]
    mapped, target_dual = publish(finish(own_g, sums))
    return source_dual.reshape(-1), target_dual.reshape(-1), mapped


def solution(mesh):
    fine = Mesh(mesh.devices.reshape(4, 4, 2, 4), ("y", "z", "core", "tgt"))
    sources = ("y", "z", "core")
    return jax.shard_map(
        body,
        mesh=fine,
        in_specs=(P(None, sources), P(None, "tgt")),
        out_specs=(P(sources), P("tgt"), P(None, "tgt")),
        check_vma=False,
    )
```

```python
import functools
import math

import jax
import jax.numpy as jnp
from jax import lax
from jax.experimental import pallas as pl
from jax.experimental.pallas import tpu as pltpu
from jax.sharding import Mesh
from jax.sharding import PartitionSpec as P

EPSILON = 0.5
LOG2E = 1.4426950408889634
UNIT = LOG2E / EPSILON
BF = jnp.bfloat16
F32 = jnp.float32
DEPTH = 256
VMEM_LIMIT = 56 * 2**20


def params():
    return pltpu.CompilerParams(vmem_limit_bytes=VMEM_LIMIT)


def log2(a):
    return jnp.log(a) * LOG2E


def split3(a):
    a1 = a.astype(BF)
    rest = a - a1.astype(F32)
    a2 = rest.astype(BF)
    rest = rest - a2.astype(F32)
    return a1, a2, rest.astype(BF)


def square_norm(points):
    return jnp.sum(points * points, axis=0, keepdims=True)


def build_still(points, term, out, shift=None):
    n = points.shape[1]
    p1, p2, p3 = (p.astype(F32) for p in split3(points * (2 * UNIT)))
    out[:, 0:128] = jnp.concatenate([p1, p1, p1, p2], axis=0).T.astype(BF)
    out[:, 128:256] = jnp.concatenate([p2, p3, still_terms(term, shift)], axis=0).T.astype(BF)


def still_terms(term, shift):
    n = term.shape[1]
    parts = [t.astype(F32) for t in split3(term)] + [jnp.ones((3, n), F32)]
    if shift is not None:
        parts += [t.astype(F32) for t in split3(shift)]
    return jnp.concatenate(parts + [jnp.zeros((64 - sum(p.shape[0] for p in parts), n), F32)], axis=0)


def build_moving(points, term, out):
    n = points.shape[1]
    p1, p2, p3 = split3(points)
    t1, t2, t3 = (t.astype(F32) for t in split3(term))
    for row, part in enumerate((p1, p2, p3, p1, p2, p1)):
        out[32 * row : 32 * row + 32, :] = part
    ones, zeros = jnp.ones((3, n), F32), jnp.zeros((7, n), F32)
    out[192:208, :] = jnp.concatenate([ones, t1, t2, t3, ones, zeros], axis=0).astype(BF)


def quarter(y_ref, t, tile):
    start = lax.axis_index("y") * (y_ref.shape[1] // 4) + t * tile
    return y_ref[:, pl.ds(pl.multiple_of(start, tile), tile)]


def tree(op, items):
    items = list(items)
    while len(items) > 1:
        items = [op(a, b) for a, b in zip(items[::2], items[1::2])] + items[len(items) & ~1 :]
    return items[0]


def lanes(block):
    return jnp.concatenate([block[k : k + 1, :] for k in range(block.shape[0])], axis=1)


def rows(line):
    return jnp.concatenate([line[:, k : k + 128] for k in range(0, line.shape[1], 128)], axis=0)


def sweep(steps, make, multiply, process):
    make(0, 0)
    multiply(0)
    make(1, 1)

    def pair(t, carry):
        multiply(1)
        make(lax.rem(2 * t + 2, steps), 0)
        process(2 * t, 0)
        multiply(0)
        make(lax.rem(2 * t + 3, steps), 1)
        process(2 * t + 1, 1)
        return carry

    lax.fori_loop(0, steps // 2, pair, 0)


def near(arrays):
    return [pltpu.with_memory_space_constraint(a, pltpu.VMEM) for a in arrays]


def whole(count):
    return [pl.BlockSpec(memory_space=pltpu.VMEM)] * count


def kept(*shapes):
    return tuple(pltpu.VMEM(shape, F32) for shape in shapes)


def row_first_kernel(tile, x_far, y_far, out, y_ref, x_ref, still, moving, scores, peak, total, sem):
    count = x_ref.shape[1]
    steps = y_ref.shape[1] // tile
    ahead = tile
    get_x = pltpu.make_async_copy(x_far, x_ref, sem.at[0])
    get_first = pltpu.make_async_copy(y_far.at[:, 0:ahead], y_ref.at[:, 0:ahead], sem.at[1])
    get_rest = pltpu.make_async_copy(y_far.at[:, ahead:], y_ref.at[:, ahead:], sem.at[2])
    get_x.start()
    get_first.start()
    get_rest.start()
    get_x.wait()
    x = x_ref[...]
    norm = -UNIT * square_norm(x)
    build_still(x, norm, still)
    moving[:, 208:DEPTH, :] = jnp.zeros((2, DEPTH - 208, tile), BF)
    peak[...] = jnp.zeros(peak.shape, F32)
    total[...] = jnp.zeros(total.shape, F32)

    def make(t, slot):
        y = y_ref[:, pl.ds(pl.multiple_of(t * tile, tile), tile)]
        build_moving(y, -UNIT * square_norm(y), moving.at[slot])

    def multiply(slot):
        scores[slot] = jnp.dot(still[...], moving[slot], preferred_element_type=F32)

    get_first.wait()
    make(0, 0)
    sample = jnp.dot(still[...], moving[0, :, 0:256], preferred_element_type=F32)
    base = jnp.max(jnp.maximum(sample[:, 0:128], sample[:, 128:256]).T, axis=0, keepdims=True)
    _, p2, p3 = split3(x * (2 * UNIT))
    terms = still_terms(norm, -base)
    still[:, 128:256] = jnp.concatenate([p2.astype(F32), p3.astype(F32), terms], axis=0).T.astype(BF)

    def process(t, slot):
        for r in range(0, count, 8):
            e = [jnp.exp2(scores[slot, r : r + 8, k : k + 128]) for k in range(0, tile, 128)]
            total[r : r + 8, :] += tree(jnp.add, e)

    get_rest.wait()
    sweep(steps, make, multiply, process)

    @pl.when(jnp.max(total[...]) > 1e34)
    def _():
        peak[...] = jnp.full(peak.shape, -1e30, F32)
        total[...] = jnp.zeros(total.shape, F32)

        def step(t, carry):
            make(t, 0)
            multiply(0)
            for r in range(0, count, 8):
                s = [scores[0, r : r + 8, k : k + 128] for k in range(0, tile, 128)]
                old = peak[r : r + 8, :]
                new = jnp.maximum(old, tree(jnp.maximum, s))
                part = tree(jnp.add, [jnp.exp2(a - new) for a in s])
                total[r : r + 8, :] = total[r : r + 8, :] * jnp.exp2(old - new) + part
                peak[r : r + 8, :] = new
            return carry

        lax.fori_loop(0, steps, step, 0)

    peaks = peak[...].T
    top = jnp.max(peaks, axis=0, keepdims=True)
    whole = jnp.sum(total[...].T * jnp.exp2(peaks - top), axis=0, keepdims=True)
    pair = jnp.concatenate([rows(top + base), rows(whole)], axis=0)
    share = x_ref[pl.ds(pl.multiple_of(8 * lax.axis_index("tgt"), 8), 8), :]
    for s in range(out.shape[0]):
        out[s, 0:8] = pair
        for k in range(0, count, 128):
            out[s, 8 + k // 16 : 16 + k // 16] = share[:, k : k + 128]


def row_first(x, y, copies):
    tile, count = 2048, x.shape[1]
    return pl.pallas_call(
        functools.partial(row_first_kernel, tile),
        in_specs=[pl.BlockSpec(memory_space=pl.ANY)] * 2,
        out_specs=whole(2),
        out_shape=kept((copies, 8 + count // 16, 128), y.shape),
        scratch_shapes=[
            pltpu.VMEM(x.shape, F32),
            pltpu.VMEM((count, DEPTH), BF),
            pltpu.VMEM((2, DEPTH, tile), BF),
            pltpu.VMEM((2, count, tile), F32),
            pltpu.VMEM((count, 128), F32),
            pltpu.VMEM((count, 128), F32),
            pltpu.SemaphoreType.DMA((3,)),
        ],
        compiler_params=params(),
        name="row_first",
    )(x, y)


def col_first_kernel(tile, log_b, parts, y_ref, out, dual_out, x_out, still, moving, scores, found):
    count = x_out.shape[2]
    half, group = found.shape[0] // 2, tile // 128
    for row in range(4):
        pieces = [parts[4 * s + row] for s in range(4)]
        top = tree(jnp.maximum, [p[0:4] for p in pieces])
        total = tree(jnp.add, [p[4:8] * jnp.exp2(p[0:4] - top) for p in pieces])
        dual = -(top + log2(total) + log_b)
        dual_out[4 * row : 4 * row + 4, :] = dual
        shares = [jnp.concatenate([p[k : k + 8] for k in range(8, p.shape[0], 8)], axis=1) for p in pieces]
        x = jnp.concatenate(shares, axis=0)
        x_out[row] = x
        build_still(x, lanes(dual) - UNIT * square_norm(x), still.at[pl.ds(count * row, count)])
    moving[:, 208:DEPTH, :] = jnp.zeros((2, DEPTH - 208, tile), BF)

    def make(t, slot):
        y = quarter(y_ref, t, tile)
        build_moving(y, -UNIT * square_norm(y), moving.at[slot])

    def multiply(slot):
        scores[slot] = jnp.dot(still[...], moving[slot], preferred_element_type=F32)

    def process(t, slot):
        for k in range(0, tile, 128):
            column = slice(k, k + 128)
            total = [jnp.exp2(scores[slot, 8 * q : 8 * q + 8, column]) for q in range(8)]
            for r in range(64, 4 * count, 64):
                total = [a + jnp.exp2(scores[slot, r + 8 * q : r + 8 * q + 8, column]) for q, a in enumerate(total)]
            found[pl.ds(half + group * t + k // 128, 1), :] = jnp.sum(tree(jnp.add, total), axis=0, keepdims=True)

    found[0:half, :] = jnp.zeros((half, 128), F32)
    steps = y_ref.shape[1] // 4 // tile
    sweep(steps, make, multiply, process)

    @pl.when(jnp.min(found[half:, :]) < 1e-25)
    def _():
        def step(t, carry):
            make(t, 0)
            multiply(0)
            for k in range(0, tile, 128):
                peak = jnp.full((8, 128), -1e30, F32)
                total = jnp.zeros((8, 128), F32)
                for r in range(0, 4 * count, 128):
                    s = [scores[0, r + q : r + q + 8, k : k + 128] for q in range(0, 128, 8)]
                    new = jnp.maximum(peak, tree(jnp.maximum, s))
                    total = total * jnp.exp2(peak - new) + tree(jnp.add, [jnp.exp2(a - new) for a in s])
                    peak = new
                best = jnp.max(peak, axis=0, keepdims=True)
                found[pl.ds(group * t + k // 128, 1), :] = best
                whole = jnp.sum(total * jnp.exp2(peak - best), axis=0, keepdims=True)
                found[pl.ds(half + group * t + k // 128, 1), :] = whole
            return carry

        lax.fori_loop(0, steps, step, 0)

    line = found[0:half] + log2(found[half:])
    for s in range(out.shape[0]):
        out[s] = line


def col_first(parts, y, log_b, count, copies):
    tile, width = 512, y.shape[1] // 4
    lines = width // 64
    return pl.pallas_call(
        functools.partial(col_first_kernel, tile, log_b),
        in_specs=whole(2),
        out_specs=whole(3),
        out_shape=kept((copies, lines // 2, 128), (16, 128), (4, 32, count)),
        scratch_shapes=[
            pltpu.VMEM((4 * count, DEPTH), BF),
            pltpu.VMEM((2, DEPTH, tile), BF),
            pltpu.VMEM((2, 4 * count, tile), F32),
            pltpu.VMEM((lines, 128), F32),
        ],
        compiler_params=params(),
        name="col_first",
    )(*near([parts, y]))


def row_second_kernel(tile, log_a, log_b, x_ref, f_ref, y_ref, parts, *rest):
    out, own, every, still, moving, scores, total, dual = rest
    count = x_ref.shape[2]
    half = parts.shape[1]
    logs = [parts[s] for s in range(parts.shape[0])]
    top = tree(jnp.maximum, logs)
    g = -(top + log2(tree(jnp.add, [jnp.exp2(p - top) for p in logs])) + log_a)
    every[...] = g
    for t in range(half // 4):
        dual[t] = g[4 * t : 4 * t + 4]
    own[...] = dual[lax.axis_index(("z", "core"))]
    for row in range(4):
        x = x_ref[row]
        f = lanes(f_ref[4 * row : 4 * row + 4])
        build_still(x, f - UNIT * square_norm(x), still.at[pl.ds(count * row, count)])
    moving[:, 208:DEPTH, :] = jnp.zeros((2, DEPTH - 208, tile), BF)
    total[...] = jnp.zeros(total.shape, F32)

    def make(t, slot):
        y = quarter(y_ref, t, tile)
        build_moving(y, lanes(dual[t]) + log_b - UNIT * square_norm(y), moving.at[slot])

    def multiply(slot):
        scores[slot] = jnp.dot(still[...], moving[slot], preferred_element_type=F32)

    def process(t, slot):
        for r in range(0, 4 * count, 8):
            e = [jnp.exp2(scores[slot, r : r + 8, k : k + 128]) for k in range(0, tile, 128)]
            total[r : r + 8, :] += tree(jnp.add, e)

    sweep(y_ref.shape[1] // 4 // tile, make, multiply, process)
    for k in range(4):
        line = jnp.sum(total[count * k : count * k + count, :].T, axis=0, keepdims=True)
        for s in range(out.shape[0]):
            out[s, k] = rows(line)


def row_second(x, f, y, parts, log_a, log_b, copies):
    tile, count, width = 512, x.shape[2], y.shape[1] // 4
    return pl.pallas_call(
        functools.partial(row_second_kernel, tile, log_a, log_b),
        in_specs=whole(4),
        out_specs=whole(3),
        out_shape=kept((copies, 4, 4, 128), (4, 128), (width // 128, 128)),
        scratch_shapes=[
            pltpu.VMEM((4 * count, DEPTH), BF),
            pltpu.VMEM((2, DEPTH, tile), BF),
            pltpu.VMEM((2, 4 * count, tile), F32),
            pltpu.VMEM((4 * count, 128), F32),
            pltpu.VMEM((width // tile, tile // 128, 128), F32),
        ],
        compiler_params=params(),
        name="row_second",
    )(*near([x, f, y, parts]))


def col_second_kernel(tile, log_a, x_ref, f_ref, parts, y_ref, g_ref, mine, other, own, *rest):
    still, moving, scores, weights, values, dual, out, fresh = rest
    count = x_ref.shape[2]
    half = 4 * count
    for row in range(4):
        sums = tree(jnp.add, [parts[s, row] for s in range(parts.shape[0])])
        f = f_ref[4 * row : 4 * row + 4, :] - log2(sums)
        fresh[row] = f * (1.0 / UNIT)
        x = x_ref[row]
        here = slice(count * row, count * row + count)
        there = slice(half + count * row, half + count * row + count)
        build_still(x, lanes(f) - UNIT * square_norm(x), still.at[here])
        for part, piece in enumerate(split3(x)):
            values[32 * part : 32 * part + 32, here] = piece
            values[32 * part : 32 * part + 32, there] = piece
    own[...] = fresh[lax.axis_index("y")]
    values[96:112, :] = jnp.ones((16, 2 * half), BF)
    moving[:, 208:DEPTH, :] = jnp.zeros((2, DEPTH - 208, tile), BF)
    weights[1] = jnp.zeros((2 * half, tile), BF)
    out[:, 128:136, :] = jnp.zeros((out.shape[0], 8, 128), F32)
    for t in range(dual.shape[0]):
        dual[t] = g_ref[2 * t : 2 * t + 2, :]

    def make(t, slot):
        y = quarter(y_ref, t, tile)
        build_moving(y, lanes(dual[t]) + log_a - UNIT * square_norm(y), moving.at[slot])

    def multiply(slot):
        scores[slot] = jnp.dot(still[...], moving[slot], preferred_element_type=F32)

    def weigh(slot):
        for r in range(0, half, 16):
            for k in range(0, tile, 128):
                e = jnp.exp2(scores[slot, r : r + 16, k : k + 128])
                high = e.astype(BF)
                weights[slot, r : r + 16, k : k + 128] = high
                weights[slot, half + r : half + r + 16, k : k + 128] = (e - high.astype(F32)).astype(BF)

    def gather(block, slot):
        sums = jnp.dot(values[...], weights[slot], preferred_element_type=F32)
        moment = sums[0:32] + sums[32:64] + sums[64:96]
        for h in range(2):
            k = 2 * slot + h
            out[block, 32 * k : 32 * k + 32, :] = moment[:, 128 * h : 128 * h + 128]
            out[block, 128 + k : 129 + k, :] = sums[96:97, 128 * h : 128 * h + 128]

    steps = y_ref.shape[1] // 4 // tile
    make(0, 0)
    multiply(0)
    make(1, 1)

    def pair(t, carry):
        multiply(1)
        make(lax.rem(2 * t + 2, steps), 0)
        gather(lax.rem(t + steps // 2 - 1, steps // 2), 1)
        weigh(0)
        multiply(0)
        make(lax.rem(2 * t + 3, steps), 1)
        gather(t, 0)
        weigh(1)
        return carry

    lax.fori_loop(0, steps // 2, pair, 0)
    gather(steps // 2 - 1, 1)
    core = lax.axis_index("core")
    for z in range(mine.shape[0]):
        mine[z] = out[2 * z + core]
        other[z] = out[2 * z + 1 - core]


def col_second(x, f, parts, y, g, log_a):
    tile, count, width = 256, x.shape[2], y.shape[1] // 4
    return pl.pallas_call(
        functools.partial(col_second_kernel, tile, log_a),
        in_specs=whole(5),
        out_specs=whole(2) + [pl.BlockSpec((4, 128), lambda: (0, 0))],
        out_shape=kept(*((width // 1024, 136, 128),) * 2) + (jax.ShapeDtypeStruct((4, 128), F32),),
        scratch_shapes=[
            pltpu.VMEM((4 * count, DEPTH), BF),
            pltpu.VMEM((2, DEPTH, tile), BF),
            pltpu.VMEM((2, 4 * count, tile), F32),
            pltpu.VMEM((2, 8 * count, tile), BF),
            pltpu.VMEM((112, 8 * count), BF),
            pltpu.VMEM((width // tile, 2, 128), F32),
            pltpu.VMEM((width // 512, 136, 128), F32),
            pltpu.VMEM((4, 4, 128), F32),
        ],
        compiler_params=params(),
        name="col_second",
    )(*near([x, f, parts, y, g]))


def merge_kernel(mine, other, *outs):
    for k, out in enumerate(outs):
        z = (lax.axis_index("z") + k) & 3
        out[...] = mine[z] + other[z]


def merge(mine, other):
    return pl.pallas_call(
        merge_kernel,
        in_specs=whole(2),
        out_specs=whole(4),
        out_shape=kept(*((136, 128),) * 4),
        compiler_params=params(),
        name="merge",
    )(*near([mine, other]))


def finish_kernel(g_ref, p0, p1, p2, p3, out):
    sums = (p0[...] + p1[...]) + (p2[...] + p3[...])
    for k in range(4):
        out[32 * k : 32 * k + 32, :] = sums[32 * k : 32 * k + 32] / sums[128 + k : 129 + k]
    dual = (g_ref[...] - log2(sums[128:132])) * (1.0 / UNIT)
    out[128:136, :] = jnp.concatenate([dual, dual], axis=0)


def finish(g, parts):
    return pl.pallas_call(
        finish_kernel,
        in_specs=whole(5),
        out_specs=whole(1)[0],
        out_shape=kept((136, 128))[0],
        compiler_params=params(),
        name="finish",
    )(*near([g, *parts]))


TURNS = (0, 1, 3, 2)


def place_kernel(turns, *refs):
    mapped, dual = refs[-2:]
    y, z, core = lax.axis_index("y"), lax.axis_index("z"), lax.axis_index("core")
    for n, ref in enumerate(refs[:-2]):
        turn, owner = turns[n // 2], core if n % 2 == 0 else 1 - core
        for b in range(4):
            row = jnp.where(owner == 0, y - TURNS[b], y - turn) & 3
            column = jnp.where(owner == 0, z - turn, z - TURNS[b]) & 3
            spot = row * 8 + column * 2 + owner
            for k in range(4):
                where = pl.ds(pl.multiple_of(512 * spot + 128 * k, 128), 128)
                mapped[:, where] = ref[b, 32 * k : 32 * k + 32, :]
            dual[spot] = ref[b, 128:132, :]


def place(pieces, turns):
    return pl.pallas_call(
        functools.partial(place_kernel, turns),
        in_specs=whole(len(pieces)),
        out_shape=(jax.ShapeDtypeStruct((32, 16384), F32), jax.ShapeDtypeStruct((32, 4, 128), F32)),
        compiler_params=params(),
        name="place",
    )(*near(pieces))


def turned(block, turn, first):
    pairs = []
    for y in range(4):
        for z in range(4):
            for core in range(2):
                along_y = (core == 0) == first
                to = ((y + turn) % 4, z) if along_y else (y, (z + turn) % 4)
                pairs.append((8 * y + 2 * z + core, 8 * to[0] + 2 * to[1] + core))
    return lax.ppermute(block, ("y", "z", "core"), pairs)


def publish(block):
    line = jnp.stack([block] + [turned(block, turn, True) for turn in TURNS[1:]])
    turns = (0, 3, 1, 2)
    pieces = [line] + [turned(line, turn, False) for turn in turns[1:]]
    others = [lax.ppermute(piece, "core", [(0, 1), (1, 0)]) for piece in pieces]
    return place([p for pair in zip(pieces, others) for p in pair], turns)


def spread(copies, axes):
    return lax.all_to_all(copies, axes, 0, 0)


def along(block, axis, turn):
    n = lax.axis_size(axis)
    return lax.ppermute(block, axis, [(i, (i + turn) % n) for i in range(n)])


def body(x, y):
    log_a = -math.log2(x.shape[1] * 32)
    log_b = -math.log2(y.shape[1] * 4)
    first, near_y = row_first(x, y, 16)
    partial, f1, near_x = col_first(spread(first, ("tgt", "y")), near_y, log_b, x.shape[1], 8)
    partial = spread(partial, ("z", "core"))
    second, own_g, g1 = row_second(near_x, f1, near_y, partial, log_a, log_b, 16)
    mine, other, source_dual = col_second(near_x, f1, spread(second, ("tgt", "y")), near_y, g1, log_a)
    sums = merge(mine, along(other, "core", 1))
    sums = [sums[0]] + [along(sums[turn], "z", turn) for turn in (2, 1, 3)]
    mapped, target_dual = publish(finish(own_g, sums))
    return source_dual.reshape(-1), target_dual.reshape(-1), mapped


def solution(mesh):
    fine = Mesh(mesh.devices.reshape(4, 4, 2, 4), ("y", "z", "core", "tgt"))
    sources = ("y", "z", "core")
    return jax.shard_map(
        body,
        mesh=fine,
        in_specs=(P(None, sources), P(None, "tgt")),
        out_specs=(P(sources), P("tgt"), P(None, "tgt")),
        check_vma=False,
    )
```
